512 devices in a mesh: gx: 8 (over z_lo, core), gy: 8 (over y), gz: 8 (over x, z_hi).
Axes of the slice: x: 4, y: 8, z: 8 (z_hi: 2, z_lo: 4; z = z_hi * 4 + z_lo), core: 2. Of those that a mesh axis runs over, the one named last changes fastest.
Arguments:
- positions: float32 [3, 8, 8, 8, 32], P(None, 'gx', 'gy', 'gz'), as said below
- species: int32 [8, 8, 8, 32], P('gx', 'gy', 'gz'), may hold values from 0 to 88
- atom_count: int32 [8, 8, 8], P('gx', 'gy', 'gz'), may hold values from 16 to 32, as said below
- edge_count: int32 [8, 8, 8], P('gx', 'gy', 'gz'), may hold values from 0 to 1792, as said below
- sender: int32 [8, 8, 8, 1792], P('gx', 'gy', 'gz'), may hold values from 0 to 863, as said below
- receiver: int32 [8, 8, 8, 1792], P('gx', 'gy', 'gz'), may hold values from 0 to 31, as said below
- image_shift: int32 [3, 8, 8, 8, 1792], P(None, 'gx', 'gy', 'gz'), may hold values from -1 to 1, as said below
- embed: float32 [89, 128], replicated, may hold values from -6 to 6
- radial_in: float32 [2, 8, 64], replicated, may hold values from -2 to 2
- radial_out: float32 [2, 64, 384], replicated, may hold values from -0.75 to 0.75
- w_up: float32 [2, 128, 128], replicated, may hold values from -0.5 to 0.5
- lam: float32 [2, 2, 128], replicated, may hold values from -4 to 4
- w_mix: float32 [2, 128, 128], replicated, may hold values from -0.5 to 0.5
- read_one: float32 [128], replicated, may hold values from -0.5 to 0.5
- read_hidden: float32 [128, 16], replicated, may hold values from -0.5 to 0.5
- read_out: float32 [16], replicated, may hold values from -1.5 to 1.5
Outputs:
- site_energy: float32 [8, 8, 8, 32], P('gx', 'gy', 'gz')
- forces: float32 [3, 8, 8, 8, 32], P(None, 'gx', 'gy', 'gz')
The draws below stay inside these ranges and needn't reach their ends.
Inputs may be any that keep to these rules, and one draw needn't show every extreme that they name: `atom_count`: slots at and above a brick's count are empty: no edge names them, and their species and positions are placeholders. At least one brick is full. `edge_count`: some brick has all 1792 edge slots live. A live edge names an owned slot of the neighbour block; sender and receiver are 0 on edges that are not live. Each live edge's image-shifted sender lies within 5.5 angstrom of its receiver; every pair of owned atoms within 5 angstrom of each other, over all periodic images, is a live edge of the receiver's brick; the (sender image, receiver) pairs within a brick are distinct. A live edge's receiver is below atom_count. `image_shift`: nonzero only where the neighbour block lies across the box's boundary; 0 on edges that are not live. `positions`: any two atoms are at least 1 angstrom apart.
All inputs are finite; a program needn't handle non-finite values.
Results may differ from the reference program's by a relative error of at most 0.0085.
Values may be sent and summed in bfloat16 or wider, within the bound.
No kernel may reach another device: no remote copies, remote signals or barrier semaphores. Data moves between devices by JAX's collectives and lax.ppermute only.
A program may use at most 128 MiB of HBM per device.

```python
import jax
import jax.numpy as jnp
import numpy as np
from jax import lax

C = 128
NSPEC = 89
NB = 8
RH = 64
RO = 16
ATOMS_DEV = 32
EDGES_DEV = 1792
BRICKS_X = 8
BRICKS_Y = 8
BRICKS_Z = 8


lattice_step = 2.25


jitter_reach = 0.15


near_table = np.array([[a, b, c] for a in (-2, -1, 0, 1, 2) for b in (-2, -1, 0, 1, 2) for c in (-2, -1, 0, 1, 2) if 0 < a * a + b * b + c * c <= 5], dtype=np.int32)


def structure(key):
    count_x, count_y, count_z = (BRICKS_X, BRICKS_Y, BRICKS_Z)
    atoms = ATOMS_DEV
    depth = atoms // 16
    bricks = count_x * count_y * count_z
    near_total = near_table.shape[0]
    key_count, key_centre, key_order = jax.random.split(key, 3)
    counts = jax.random.randint(key_count, (count_x, count_y, count_z), atoms // 2, atoms + 1)
    centre = jax.random.randint(key_centre, (3,), 0, jnp.array([count_x, count_y, count_z], jnp.int32))
    index_x = jnp.arange(count_x, dtype=jnp.int32)[:, None, None]
    index_y = jnp.arange(count_y, dtype=jnp.int32)[None, :, None]
    index_z = jnp.arange(count_z, dtype=jnp.int32)[None, None, :]

    def nearby(idx, mid, total):
        gap = jnp.mod(idx - mid, total)
        return (gap <= 1) | (gap >= total - 1)
    dense = nearby(index_x, centre[0], count_x) & nearby(index_y, centre[1], count_y) & nearby(index_z, centre[2], count_z)
    counts = jnp.where(dense, atoms, counts).reshape(bricks).astype(jnp.int32)
    scores = jax.random.randint(key_order, (bricks, atoms), 0, 1 << 20) * atoms + jnp.arange(atoms, dtype=jnp.int32)[None, :]
    cell_of_slot = jnp.argsort(scores, axis=1).astype(jnp.int32)
    slot_of_cell = jnp.argsort(cell_of_slot, axis=1).astype(jnp.int32)
    index = jnp.arange(bricks, dtype=jnp.int32)
    brick_x = index // (count_y * count_z)
    brick_y = index // count_z % count_y
    brick_z = index % count_z
    cell_x = cell_of_slot // (4 * depth)
    cell_y = cell_of_slot // depth % 4
    cell_z = cell_of_slot % depth
    lattice = jnp.stack([brick_x[:, None] * 4 + cell_x, brick_y[:, None] * 4 + cell_y, brick_z[:, None] * depth + cell_z])
    brick_len = jnp.array([4, 4, depth], jnp.int32)[:, None, None, None]
    spans = jnp.array([4 * count_x, 4 * count_y, depth * count_z], jnp.int32)[:, None, None, None]
    offsets = jnp.array(near_table).T[:, None, None, :]
    moved = lattice[..., None] + offsets
    step = jnp.floor_divide(moved, brick_len) - jnp.floor_divide(lattice[..., None], brick_len)
    wrapped = jnp.floor_divide(moved, spans)
    inside = moved - wrapped * spans
    near_brick = (inside[0] // 4 * count_y + inside[1] // 4) * count_z + inside[2] // depth
    near_cell = (inside[0] % 4 * 4 + inside[1] % 4) * depth + inside[2] % depth
    near_slot = slot_of_cell[near_brick, near_cell]
    live = (near_slot < counts[near_brick]) & (jnp.arange(atoms, dtype=jnp.int32)[None, :, None] < counts[:, None, None])
    block = (step[0] + 1) * 9 + (step[1] + 1) * 3 + (step[2] + 1)
    senders = (block * atoms + near_slot).reshape(bricks, atoms * near_total)
    receivers = jnp.broadcast_to(jnp.arange(atoms, dtype=jnp.int32)[None, :, None], (bricks, atoms, near_total)).reshape(bricks, atoms * near_total)
    shifts = wrapped.reshape(3, bricks, atoms * near_total)
    live = live.reshape(bricks, atoms * near_total)
    order = jnp.argsort(jnp.where(live, 0, 1) * (atoms * near_total) + jnp.arange(atoms * near_total, dtype=jnp.int32)[None, :], axis=1)
    live_sorted = jnp.take_along_axis(live, order, axis=1)
    senders = jnp.where(live_sorted, jnp.take_along_axis(senders, order, axis=1), 0)
    receivers = jnp.where(live_sorted, jnp.take_along_axis(receivers, order, axis=1), 0)
    shifts = jnp.where(live_sorted[None], jnp.take_along_axis(shifts, order[None], axis=2), 0)
    edge_total = jnp.sum(live_sorted.astype(jnp.int32), axis=1)
    return (counts, lattice, senders, receivers, shifts, edge_total)


def draw_positions(key, part):
    counts, lattice, senders, receivers, shifts, edge_total = structure(key)
    key = jax.random.fold_in(key, 5)
    shape = lattice.shape
    jitter = jitter_reach * jnp.tanh(jax.random.normal(key, shape, jnp.float32))
    coords = (lattice.astype(jnp.float32) + 0.5) * lattice_step + jitter
    return coords.reshape(3, BRICKS_X, BRICKS_Y, BRICKS_Z, ATOMS_DEV).astype(jnp.float32)


def draw_atom_count(key, part):
    counts, lattice, senders, receivers, shifts, edge_total = structure(key)
    return counts.reshape(BRICKS_X, BRICKS_Y, BRICKS_Z)


def draw_edge_count(key, part):
    counts, lattice, senders, receivers, shifts, edge_total = structure(key)
    return edge_total.reshape(BRICKS_X, BRICKS_Y, BRICKS_Z).astype(jnp.int32)


def draw_sender(key, part):
    counts, lattice, senders, receivers, shifts, edge_total = structure(key)
    return senders.reshape(BRICKS_X, BRICKS_Y, BRICKS_Z, EDGES_DEV).astype(jnp.int32)


def draw_receiver(key, part):
    counts, lattice, senders, receivers, shifts, edge_total = structure(key)
    return receivers.reshape(BRICKS_X, BRICKS_Y, BRICKS_Z, EDGES_DEV).astype(jnp.int32)


def draw_image_shift(key, part):
    counts, lattice, senders, receivers, shifts, edge_total = structure(key)
    return shifts.reshape(3, BRICKS_X, BRICKS_Y, BRICKS_Z, EDGES_DEV).astype(jnp.int32)


def place_ends(values, rng, smallest, top_value):
    spot = [jax.random.randint(jax.random.fold_in(rng, axis), (), 0, length) for axis, length in enumerate(values.shape)]
    longest = values.shape.index(max(values.shape))
    next_to = spot[:longest] + [(spot[longest] + 1) % values.shape[longest]] + spot[longest + 1:]
    return values.at[tuple(spot)].set(smallest).at[tuple(next_to)].set(top_value)


def normal_values(stream_key, dims, scale, bound, held_as=jnp.bfloat16):
    return jnp.clip(scale * jax.random.normal(stream_key, dims, jnp.float32), -bound, bound).astype(held_as)


def setup_inputs(seed: int = 0) -> dict:
    arg_keys = jax.random.split(jax.random.key(seed), 17)
    positions = draw_positions(jax.random.fold_in(arg_keys[16], 71), 0)
    species = place_ends(jax.random.randint(arg_keys[1], (BRICKS_X, BRICKS_Y, BRICKS_Z, ATOMS_DEV), 0, NSPEC), jax.random.fold_in(arg_keys[1], 1), 0, NSPEC - 1).astype(jnp.int32)
    atom_count = draw_atom_count(jax.random.fold_in(arg_keys[16], 71), 0)
    edge_count = draw_edge_count(jax.random.fold_in(arg_keys[16], 71), 0)
    sender = draw_sender(jax.random.fold_in(arg_keys[16], 71), 0)
    receiver = draw_receiver(jax.random.fold_in(arg_keys[16], 71), 0)
    image_shift = draw_image_shift(jax.random.fold_in(arg_keys[16], 71), 0)
    embed = normal_values(arg_keys[7], (NSPEC, C), 1.0, 6.0, jnp.float32)
    radial_in = normal_values(arg_keys[8], (2, NB, RH), NB ** -0.5, 2.0, jnp.float32)
    radial_out = normal_values(arg_keys[9], (2, RH, 3 * C), RH ** -0.5, 0.75, jnp.float32)
    w_up = normal_values(arg_keys[10], (2, C, C), C ** -0.5, 0.5, jnp.float32)
    lam = normal_values(arg_keys[11], (2, 2, C), 1.0, 4.0, jnp.float32)
    w_mix = normal_values(arg_keys[12], (2, C, C), C ** -0.5, 0.5, jnp.float32)
    read_one = normal_values(arg_keys[13], (C,), C ** -0.5, 0.5, jnp.float32)
    read_hidden = normal_values(arg_keys[14], (C, RO), C ** -0.5, 0.5, jnp.float32)
    read_out = normal_values(arg_keys[15], (RO,), RO ** -0.5, 1.5, jnp.float32)
    return {"positions": positions, "species": species, "atom_count": atom_count, "edge_count": edge_count, "sender": sender, "receiver": receiver, "image_shift": image_shift, "embed": embed, "radial_in": radial_in, "radial_out": radial_out, "w_up": w_up, "lam": lam, "w_mix": w_mix, "read_one": read_one, "read_hidden": read_hidden, "read_out": read_out}


cutoff_radius = 5.0
lattice_step = 2.25
mean_degree = 8.0

def rounded(value):
    kept = lax.optimization_barrier(value.astype(jnp.bfloat16)).astype(jnp.float32)
    return value + lax.stop_gradient(kept - value)

def embed_rows(embed, kinds):
    table = (kinds[:, None] == jnp.arange(embed.shape[0], dtype=jnp.int32)[None, :]).astype(jnp.float32)
    return jnp.dot(table, embed, precision=lax.Precision.HIGHEST).astype(jnp.bfloat16)

def layer(w_in, w_out, w_lift, weights_sq, w_merge, own_pos, ghost_pos, ghost_h, own_h, sender, receiver, shift_len, valid):
    atoms = own_pos.shape[1]
    width = ghost_h.shape[1]
    rel = (jnp.take(ghost_pos, sender, axis=1) + shift_len - jnp.take(own_pos, receiver, axis=1)) / cutoff_radius
    dist2 = lax.optimization_barrier(jnp.sum(rel * rel, axis=0))
    envelope = jnp.square(jnp.maximum(1.0 - dist2, 0.0)) * valid
    nbasis = w_in.shape[0]
    centres = jnp.arange(nbasis, dtype=jnp.float32) / (nbasis - 1)
    basis = jnp.exp(-jnp.square((dist2[None, :] - centres[:, None]) * nbasis))
    hidden = jax.nn.silu(lax.dot_general(basis, w_in, (((0,), (0,)), ((), ())), precision=lax.Precision.HIGHEST))
    radial = jnp.dot(hidden, w_out, precision=lax.Precision.HIGHEST) * envelope[:, None]
    lifted = jnp.take(jnp.dot(ghost_h, w_lift, precision=lax.Precision.HIGHEST), sender, axis=0)
    xpos, ypos, zpos = (rel[0], rel[1], rel[2])
    harmonics = jnp.stack([jnp.ones_like(xpos), 3.0 ** 0.5 * xpos, 3.0 ** 0.5 * ypos, 3.0 ** 0.5 * zpos, 15.0 ** 0.5 * xpos * ypos, 15.0 ** 0.5 * ypos * zpos, 15.0 ** 0.5 * xpos * zpos, 0.5 * 15.0 ** 0.5 * (xpos * xpos - ypos * ypos), 0.5 * 5.0 ** 0.5 * (2.0 * zpos * zpos - xpos * xpos - ypos * ypos)])
    onehot = (receiver[None, :] == jnp.arange(atoms, dtype=jnp.int32)[:, None]).astype(jnp.float32)
    pooling = onehot[None, :, :] * harmonics[:, None, :] / mean_degree
    base_zero = radial[:, :width] * lifted
    base_one = radial[:, width:2 * width] * lifted
    base_two = radial[:, 2 * width:] * lifted
    scalar = jnp.dot(pooling[0], base_zero, precision=lax.Precision.HIGHEST)
    order_one = jnp.einsum('mae,ec->mac', pooling[1:4], base_one, precision=lax.Precision.HIGHEST)
    order_two = jnp.einsum('mae,ec->mac', pooling[4:], base_two, precision=lax.Precision.HIGHEST)
    first = lax.optimization_barrier(jnp.sum(jnp.square(order_one), axis=0))
    second = lax.optimization_barrier(jnp.sum(jnp.square(order_two), axis=0))
    product = scalar + weights_sq[0] * first + weights_sq[1] * second
    return own_h + jnp.dot(product, w_merge, precision=lax.Precision.HIGHEST)

def readout_two(h_two, read_hidden, read_out):
    inner = jax.nn.silu(jnp.dot(h_two, read_hidden, precision=lax.Precision.HIGHEST))
    return jnp.dot(inner, read_out, precision=lax.Precision.HIGHEST)

def reference(positions, species, atom_count, edge_count, sender, receiver, image_shift, embed, radial_in, radial_out, w_up, lam, w_mix, read_one, read_hidden, read_out):
    bricks = BRICKS_X * BRICKS_Y * BRICKS_Z
    atoms = ATOMS_DEV
    edges = EDGES_DEV
    width = embed.shape[1]
    box = jnp.array([BRICKS_X * 4 * lattice_step, BRICKS_Y * 4 * lattice_step, BRICKS_Z * (atoms // 16) * lattice_step], jnp.float32)
    pos_b = positions.reshape(3, bricks, atoms).transpose(1, 0, 2)
    spec_b = species.reshape(bricks, atoms)
    send_b = sender.reshape(bricks, edges)
    recv_b = receiver.reshape(bricks, edges)
    shift_b = image_shift.reshape(3, bricks, edges).transpose(1, 0, 2).astype(jnp.float32) * box[None, :, None]
    valid_b = (jnp.arange(edges, dtype=jnp.int32)[None, :] < edge_count.reshape(bricks, 1)).astype(jnp.float32)
    mask_b = (jnp.arange(atoms, dtype=jnp.int32)[None, :] < atom_count.reshape(bricks, 1)).astype(jnp.float32)
    index = jnp.arange(bricks, dtype=jnp.int32)
    brick_x = index // (BRICKS_Y * BRICKS_Z)
    brick_y = index // BRICKS_Z % BRICKS_Y
    brick_z = index % BRICKS_Z
    columns = []
    for step_x in (-1, 0, 1):
        for step_y in (-1, 0, 1):
            for step_z in (-1, 0, 1):
                near_x = (brick_x + step_x) % BRICKS_X
                near_y = (brick_y + step_y) % BRICKS_Y
                near_z = (brick_z + step_z) % BRICKS_Z
                columns.append((near_x * BRICKS_Y + near_y) * BRICKS_Z + near_z)
    neighbours = jnp.stack(columns, axis=1).astype(jnp.int32)
    h_zero = lax.optimization_barrier(embed_rows(embed, spec_b.reshape(-1))).astype(jnp.float32).reshape(bricks, atoms, width)

    def total(pos_all):

        def first(brick):
            ghost_pos = pos_all[neighbours[brick]].transpose(1, 0, 2).reshape(3, 27 * atoms)
            ghost_h = h_zero[neighbours[brick]].reshape(27 * atoms, width)
            return layer(radial_in[0], radial_out[0], w_up[0], lam[0], w_mix[0], pos_all[brick], ghost_pos, ghost_h, h_zero[brick], send_b[brick], recv_b[brick], shift_b[brick], valid_b[brick])
        h_one = lax.map(jax.checkpoint(first), index)
        h_kept = rounded(h_one)

        def second(brick):
            ghost_pos = pos_all[neighbours[brick]].transpose(1, 0, 2).reshape(3, 27 * atoms)
            ghost_h = h_kept[neighbours[brick]].reshape(27 * atoms, width)
            return layer(radial_in[1], radial_out[1], w_up[1], lam[1], w_mix[1], pos_all[brick], ghost_pos, ghost_h, h_kept[brick], send_b[brick], recv_b[brick], shift_b[brick], valid_b[brick])
        h_two = lax.map(jax.checkpoint(second), index)
        energy_one = jnp.dot(h_one.reshape(-1, width), read_one, precision=lax.Precision.HIGHEST).reshape(bricks, atoms)
        energy_two = readout_two(h_two.reshape(-1, width), read_hidden, read_out).reshape(bricks, atoms)
        energy = (energy_one + energy_two) * mask_b
        return (jnp.sum(energy), energy)
    gradient, energy = jax.grad(total, has_aux=True)(pos_b)
    site_energy = energy.reshape(BRICKS_X, BRICKS_Y, BRICKS_Z, atoms)
    forces = (-gradient).transpose(1, 0, 2).reshape(3, BRICKS_X, BRICKS_Y, BRICKS_Z, atoms)
    return (site_energy, forces)
```

```python
import functools

import jax
import jax.numpy as jnp
import numpy as np
from jax import lax
from jax.experimental import pallas as pl
from jax.experimental.pallas import tpu as pltpu
from jax.sharding import PartitionSpec as P

cutoff_radius = 5.0
lattice_step = 2.25
AXES = ("gx", "gy", "gz")
SIDE = 8
F32 = jnp.float32
BF16 = jnp.bfloat16
S3 = 3.0**0.5
S5 = 5.0**0.5
S15 = 15.0**0.5
HIGH = lax.Precision.HIGHEST


def place(a, b, d):
    return (a * SIDE + b) * SIDE + d


def home(a, b, d):
    return place((a % 4) * 2 + d % 2, b, (d // 2) * 2 + a // 4)


def bricks():
    return [(a, b, d) for a in range(SIDE) for b in range(SIDE) for d in range(SIDE)]


def move(x, pairs):
    return lax.ppermute(x, AXES, pairs)


def bring_home(step):
    return [(place((a + step) % SIDE, b, d), home(a, b, d)) for a, b, d in bricks()]


def send_back(step):
    return [(home(a, b, d), place((a + step) % SIDE, b, d)) for a, b, d in bricks()]


def shift(axis, step):
    pairs = []
    for cell in bricks():
        other = list(cell)
        other[axis] = (other[axis] + step) % SIDE
        pairs.append((home(*other), home(*cell)))
    return pairs


def widen(x, axis):
    return [move(x, shift(axis, -1)), x, move(x, shift(axis, 1))]


def nn(a, b, **kw):
    return lax.dot_general(a, b, (((1,), (0,)), ((), ())), preferred_element_type=F32, **kw)


def nt(a, b, **kw):
    return lax.dot_general(a, b, (((1,), (1,)), ((), ())), preferred_element_type=F32, **kw)


def tn(a, b, **kw):
    return lax.dot_general(a, b, (((0,), (0,)), ((), ())), preferred_element_type=F32, **kw)


def split(x):
    hi = x.astype(BF16)
    return hi, (x - hi.astype(F32)).astype(BF16)


def stack3(x):
    hi, lo = split(x)
    return jnp.concatenate([hi, lo, hi], axis=0)


def hot(index, rows):
    edges = index.shape[1]
    return lax.broadcasted_iota(jnp.int32, (rows, edges), 0) == index


def ones_at(index, rows):
    return jnp.where(hot(index, rows), 1.0, 0.0).astype(F32)


def small_stack(x):
    hi, lo = split(x)
    hi, lo = hi.astype(F32), lo.astype(F32)
    return jnp.concatenate([hi, lo, hi, jnp.zeros_like(x)], axis=0).astype(BF16)


def hidden_units(d2, env, denv, win):
    edges = d2.shape[1]
    centre = lax.broadcasted_iota(jnp.int32, (8, edges), 0).astype(F32) * (1.0 / 7.0)
    gap = d2 - centre
    basis = jnp.exp(-64.0 * gap * gap)
    slope = basis * (-128.0 * gap)
    pre = nn(win, small_stack(basis))
    dpre = nn(win, small_stack(slope))
    sig = 1.0 / (1.0 + jnp.exp(-pre))
    act = pre * sig
    dact = sig * (1.0 + pre * (1.0 - sig)) * dpre
    return act * env, dact * env + act * denv


def call(kernel, outs, *args, flops=1_000_000, limit=40):
    return pl.pallas_call(
        kernel,
        out_shape=tuple(jax.ShapeDtypeStruct(s, d) for s, d in outs),
        compiler_params=pltpu.CompilerParams(vmem_limit_bytes=limit * 1024 * 1024),
        cost_estimate=pl.CostEstimate(flops=flops, bytes_accessed=1_000_000, transcendentals=0),
    )(*args)


def weights_kernel(embed, rin, rout, wup, emb_o, t0_o, win_o, wout_o, woutb_o, wup_o):
    emb = embed[...].astype(BF16)
    emb_o[...] = emb
    table = nn(emb.astype(F32), wup[0], precision=HIGH)
    hi, lo = split(table.T)
    t0_o[...] = jnp.concatenate([hi, lo], axis=1)
    for t in range(2):
        hi, lo = split(rin[t])
        hi, lo = hi.astype(F32), lo.astype(F32)
        both = jnp.concatenate([hi, hi, lo, jnp.zeros_like(hi)], axis=0)
        win_o[t] = both.T.astype(BF16)
        hi, lo = split(rout[t])
        woutb_o[t] = hi
        hi, lo = hi.astype(F32), lo.astype(F32)
        both = jnp.concatenate([hi, hi, lo], axis=0)
        wout_o[t] = both.T.astype(BF16)
    hi, lo = split(wup[1].T)
    wup_o[...] = jnp.concatenate([hi, lo], axis=1)


def first_kernel(
    box, left, own, right, edges, emb, t0, win, wout, lam, wmix, read_one, read_out,
    h1_o, e1_o, seed1_o, seed2_o, geo_o, pool_o, at_o, lift_o, base_o, table,
):
    count = edges.shape[1]
    table[...] = jnp.zeros_like(table)
    table[0:9] = left[...]
    table[9:18] = own[...]
    table[18:27] = right[...]
    rows = table[...]
    hi = rows.astype(BF16).astype(F32)
    rest = rows - hi
    mid = rest.astype(BF16).astype(F32)
    low = rest - mid
    parts = [
        jnp.concatenate([p[:, 32 * c : 32 * c + 32] for p in (hi, mid, low)], axis=1)
        for c in range(4)
    ]
    lhs = jnp.concatenate(parts, axis=0).astype(BF16)
    mine = jnp.concatenate([p[13:14] for p in parts] + [jnp.zeros((4, 96), F32)], axis=0)
    sender = edges[0:1]
    receiver = edges[1:2]
    slot = ones_at(jnp.bitwise_and(sender, 31), 32).astype(BF16)
    block = ones_at(jnp.right_shift(sender, 5), 32)
    recv = ones_at(receiver, 32)
    recv_b = recv.astype(BF16)
    got = nn(lhs, jnp.concatenate([slot] * 3, axis=0))
    at_recv = nn(mine.astype(BF16), jnp.concatenate([recv_b] * 3, axis=0))
    sent = [jnp.sum(got[32 * c : 32 * c + 32] * block, axis=0, keepdims=True) for c in range(4)]
    rel = []
    for c in range(3):
        d = sent[c] - at_recv[c : c + 1]
        d = d - jnp.round(d * (1.0 / box[c])) * box[c]
        rel.append(d * (1.0 / cutoff_radius))
    x, y, z = rel
    d2 = x * x + y * y + z * z
    reach = jnp.maximum(1.0 - d2, 0.0)
    env = reach * reach
    denv = -2.0 * reach
    geo_o[...] = jnp.concatenate([x, y, z, d2, env, denv, d2, d2], axis=0)
    harmonics = [
        jnp.ones_like(x),
        S3 * x,
        S3 * y,
        S3 * z,
        S15 * x * y,
        S15 * y * z,
        S15 * x * z,
        0.5 * S15 * (x * x - y * y),
        0.5 * S5 * (2.0 * z * z - x * x - y * y),
    ]
    for m, value in enumerate(harmonics):
        pool_o[32 * m : 32 * m + 32] = (recv * (value * 0.125)).astype(BF16)
    hidden, _ = hidden_units(d2, env, denv, win[0])
    radial = nn(wout[0], stack3(hidden))
    kind = ones_at(sent[3].astype(jnp.int32), 128).astype(BF16)
    lift = nn(t0[...], jnp.concatenate([kind, kind], axis=0))
    lift_o[...] = lift.astype(BF16)
    sums = []
    for order, (a, b) in enumerate(((0, 32), (32, 128), (128, 288))):
        base = (radial[128 * order : 128 * order + 128] * lift).astype(BF16)
        base_o[128 * order : 128 * order + 128] = base
        sums.append(nt(pool_o[a:b], base))
    product = sums[0]
    for order in (1, 2):
        total = sums[order]
        weight = lam[0, order - 1 : order]
        square = sum(
            total[32 * m : 32 * m + 32] * total[32 * m : 32 * m + 32]
            for m in range(2 * order + 1)
        )
        product = product + weight * square
        first = 0 if order == 1 else 96
        at_o[first : first + 32 * (2 * order + 1)] = (2.0 * weight * total).astype(BF16)
    kinds = own[4:5, 96:128]
    mask = jnp.where(kinds >= 0.0, 1.0, 0.0)
    own_kind = jnp.where(
        lax.broadcasted_iota(jnp.int32, (128, 32), 0) == kinds.astype(jnp.int32), 1.0, 0.0
    ).astype(BF16)
    h0 = tn(own_kind, emb[...])
    h1 = h0 + nn(product, wmix[0], precision=HIGH)
    h1_o[...] = h1.astype(BF16)
    e1_o[...] = nt(read_one[...], h1, precision=HIGH) * mask
    pad = jnp.zeros((7, 32), F32)
    mask8 = jnp.concatenate([mask, pad], axis=0)
    zero = lax.broadcasted_iota(jnp.int32, (8, 128), 0) == 0
    seed1_o[...] = tn(mask8, jnp.where(zero, read_one[...], 0.0), precision=HIGH)
    zero = lax.broadcasted_iota(jnp.int32, (8, 16), 0) == 0
    seed2_o[...] = tn(mask8, jnp.where(zero, read_out[...], 0.0), precision=HIGH)


def radial_kernel(edges, geo, win, wout, hot_o, rad_o, slope_o):
    sender = edges[0:1]
    for r in range(0, 864, 96):
        row = lax.broadcasted_iota(jnp.int32, (96, sender.shape[1]), 0) + r
        hot_o[r : r + 96] = jnp.where(row == sender, 1.0, 0.0).astype(BF16)
    hidden, slope = hidden_units(geo[3:4], geo[4:5], geo[5:6], win[1])
    rad_o[...] = nn(wout[1], stack3(hidden))
    slope_o[...] = slope


def direction_kernel(edges, geo, pool, at, lift, base, win, wout, v_o):
    x, y, z = geo[0:1], geo[1:2], geo[2:3]
    recv = ones_at(edges[1:2], 32)
    _, slope = hidden_units(geo[3:4], geo[4:5], geo[5:6], win[0])
    drad = nn(wout[0], stack3(slope))
    g1 = tn(at[0:96], pool[32:128])
    g2 = tn(at[96:256], pool[128:288])
    common = drad[0:128] * 0.125 + drad[128:256] * g1 + drad[256:384] * g2
    common = lift[...].astype(F32) * common
    b1 = base[128:256].astype(F32)
    b2 = base[256:384].astype(F32)
    recv8 = recv * 0.125
    turns = (
        ((0, S15 * y), (2, S15 * z), (3, S15 * x), (4, -S5 * x)),
        ((0, S15 * x), (1, S15 * z), (3, -S15 * y), (4, -S5 * y)),
        ((1, S15 * y), (2, S15 * x), (4, 2.0 * S5 * z)),
    )
    for k, coordinate in enumerate((x, y, z)):
        h1 = tn(at[32 * k : 32 * k + 32], (recv8 * S3).astype(BF16))
        left = jnp.concatenate([at[96 + 32 * m : 128 + 32 * m] for m, _ in turns[k]], axis=0)
        right = jnp.concatenate([(recv8 * f).astype(BF16) for _, f in turns[k]], axis=0)
        h2 = tn(left, right)
        v = common * (2.0 * coordinate) + b1 * h1 + b2 * h2
        v_o[128 * k : 128 * k + 128] = v.astype(BF16)


def second_kernel(
    left, own, right, hotref, rad, pool, wup, lam, wmix, read_hidden, seed2,
    dleft_o, down_o, dright_o, dh2_o, e2_o, drad_o, base_o, da_o,
):
    feats = jnp.concatenate([left[...], own[...], right[...]], axis=0)
    got = tn(feats, hotref[...]).astype(BF16)
    lift = nn(wup[...], jnp.concatenate([got, got], axis=0))
    sums = []
    spans = ((0, 32), (32, 128), (128, 288))
    for order, (a, b) in enumerate(spans):
        base = (rad[128 * order : 128 * order + 128] * lift).astype(BF16)
        base_o[128 * order : 128 * order + 128] = base
        sums.append(nt(pool[a:b], base))
    product = sums[0]
    for order in (1, 2):
        total = sums[order]
        square = sum(
            total[32 * m : 32 * m + 32] * total[32 * m : 32 * m + 32]
            for m in range(2 * order + 1)
        )
        product = product + lam[1, order - 1 : order] * square
    h2 = own[128:160].astype(F32) + nn(product, wmix[1], precision=HIGH)
    pre = nn(h2, read_hidden[...], precision=HIGH)
    sig = 1.0 / (1.0 + jnp.exp(-pre))
    inner = pre * sig
    seed = seed2[...]
    e2_o[...] = nt(jnp.ones((8, 16), F32), inner * seed, precision=HIGH)
    dpre = seed * sig * (1.0 + pre * (1.0 - sig))
    dh2 = nt(dpre, read_hidden[...], precision=HIGH)
    dh2_o[...] = dh2
    dp = nt(dh2, wmix[1], precision=HIGH)
    da_o[0:32] = dp.astype(BF16)
    for order in (1, 2):
        weight = 2.0 * lam[1, order - 1 : order] * dp
        a = spans[order][0]
        for m in range(2 * order + 1):
            piece = weight * sums[order][32 * m : 32 * m + 32]
            da_o[a + 32 * m : a + 32 * m + 32] = piece.astype(BF16)
    dlift = None
    for order, (a, b) in enumerate(spans):
        g = tn(da_o[a:b], pool[a:b])
        drad_o[128 * order : 128 * order + 128] = (lift * g).astype(BF16)
        term = rad[128 * order : 128 * order + 128] * g
        dlift = term if dlift is None else dlift + term
    hi, lo = split(dlift)
    back = nt(hotref[...], jnp.concatenate([hi, lo], axis=0))
    back = back[:, 0:128] + back[:, 128:256]
    dleft_o[...] = back[0:288].astype(BF16)
    down_o[...] = back[288:576]
    dright_o[...] = back[576:864].astype(BF16)


def slope_kernel(edges, geo, slope, drad, base, da, woutb, drel_o):
    x, y, z = geo[0:1], geo[1:2], geo[2:3]
    recv8 = ones_at(edges[1:2], 32) * 0.125
    dhidden = nn(woutb[1], drad[...])
    dd2 = 2.0 * jnp.sum(dhidden * slope[...], axis=0, keepdims=True)
    q1 = nn(da[32:128], base[128:256])
    q2 = nn(da[128:288], base[256:384])
    one = [
        jnp.sum(q1[32 * m : 32 * m + 32] * recv8, axis=0, keepdims=True) * S3 for m in range(3)
    ]
    two = [jnp.sum(q2[32 * m : 32 * m + 32] * recv8, axis=0, keepdims=True) for m in range(5)]
    dx = dd2 * x + one[0] + S15 * (two[0] * y + two[2] * z + two[3] * x) - S5 * two[4] * x
    dy = dd2 * y + one[1] + S15 * (two[0] * x + two[1] * z - two[3] * y) - S5 * two[4] * y
    dz = dd2 * z + one[2] + S15 * (two[1] * y + two[2] * x) + 2.0 * S5 * two[4] * z
    none = jnp.zeros_like(dx)
    drel_o[...] = jnp.concatenate([dx, dy, dz, none, none, none, none, none], axis=0)


def force_kernel(edges, folded, dh2, seed1, e1, e2, wup, wmix, v, drel2, left_o, own_o, right_o, rows):
    dh1 = dh2[...] + seed1[...] + nt(folded[...], wup[1], precision=HIGH)
    dp = nt(dh1, wmix[0], precision=HIGH)
    hi, lo = split(dp)
    dp2 = jnp.concatenate([hi, lo], axis=0)
    sender = edges[0:1]
    recv = ones_at(edges[1:2], 32)
    slot = ones_at(jnp.bitwise_and(sender, 31), 32).astype(BF16)
    block = ones_at(jnp.right_shift(sender, 5), 32)
    spread, pulled = [], []
    for k in range(3):
        q = nn(dp2, v[128 * k : 128 * k + 128])
        q = q[0:32] + q[32:64]
        drel = jnp.sum(q * recv, axis=0, keepdims=True) + drel2[k : k + 1]
        force = drel * (-1.0 / cutoff_radius)
        hi, lo = split(force)
        hi, lo = hi.astype(F32), lo.astype(F32)
        spread += [block * hi, block * lo]
        pulled += [hi, lo]
    pushed = nt(jnp.concatenate(spread, axis=0).astype(BF16), slot)
    pulled = jnp.concatenate(pulled + [jnp.zeros_like(hi)] * 2, axis=0).astype(BF16)
    pulled = nt(pulled, recv.astype(BF16))
    rows[...] = jnp.zeros_like(rows)
    for k in range(3):
        rows[:, 32 * k : 32 * k + 32] = pushed[64 * k : 64 * k + 32] + pushed[64 * k + 32 : 64 * k + 64]
        rows[13:14, 32 * k : 32 * k + 32] = (
            rows[13:14, 32 * k : 32 * k + 32] - pulled[2 * k : 2 * k + 1] - pulled[2 * k + 1 : 2 * k + 2]
        )
    rows[13:14, 96:128] = e1[...] + e2[0:1]
    left_o[...] = rows[0:9]
    own_o[...] = rows[9:18]
    right_o[...] = rows[18:27]


def local(
    positions, species, atom_count, edge_count, sender, receiver, image_shift,
    embed, radial_in, radial_out, w_up, lam, w_mix, read_one, read_hidden, read_out,
):
    atoms = positions.shape[-1]
    count = sender.shape[-1]
    box = (SIDE * 4 * lattice_step, SIDE * 4 * lattice_step, SIDE * (atoms // 16) * lattice_step)

    owned = jnp.arange(atoms, dtype=jnp.int32) < atom_count[0, 0, 0]
    kinds = jnp.where(owned, species[0, 0, 0], -1).astype(F32)
    row = jnp.concatenate([positions.reshape(3 * atoms), kinds])[None]
    s, r = sender[0, 0, 0], receiver[0, 0, 0]
    block, slot = s // atoms, s % atoms
    block = (block % 3) * 9 + (block // 3 % 3) * 3 + block // 9
    live = jnp.arange(count, dtype=jnp.int32) < edge_count[0, 0, 0]
    edges = jnp.stack([jnp.where(live, block * atoms + slot, 1023), jnp.where(live, r, 99)])

    padded = jnp.pad(embed, ((0, 128 - embed.shape[0]), (0, 0)))
    emb, t0, win, wout, woutb, wup = call(
        weights_kernel,
        [((128, 128), BF16), ((128, 256), BF16), ((2, 64, 32), BF16), ((2, 384, 192), BF16),
         ((2, 64, 384), BF16), ((128, 256), BF16)],
        padded, radial_in, radial_out, w_up,
    )

    line = jnp.concatenate([move(row, bring_home(d)) for d in (-1, 0, 1)], axis=0)
    edges = move(edges, bring_home(0))
    plane = jnp.concatenate(widen(line, 1), axis=0)
    left, own, right = widen(plane, 2)

    h1, e1, seed1, seed2, geo, pool, at, lift, base = pl.pallas_call(
        functools.partial(first_kernel, box),
        out_shape=tuple(
            jax.ShapeDtypeStruct(s, d)
            for s, d in (
                ((32, 128), BF16), ((1, 32), F32), ((32, 128), F32), ((32, 16), F32), ((8, count), F32),
                ((288, count), BF16), ((256, 128), BF16), ((128, count), BF16), ((384, count), BF16),
            )
        ),
        scratch_shapes=[pltpu.VMEM((32, 128), F32)],
        compiler_params=pltpu.CompilerParams(vmem_limit_bytes=40 * 1024 * 1024),
        cost_estimate=pl.CostEstimate(flops=1_000_000, bytes_accessed=1_000_000, transcendentals=0),
    )(left, own, right, edges, emb, t0, win, wout, lam, w_mix, read_one[None], read_out[None])

    line = jnp.concatenate(widen(h1, 0), axis=0)
    plane = jnp.concatenate(widen(line, 1), axis=0)
    left, own, right = widen(plane, 2)

    hotref, rad, slope = call(
        radial_kernel,
        [((864, count), BF16), ((384, count), F32), ((64, count), F32)],
        edges, geo, win, wout, flops=1_000_000_000,
    )
    (v,) = call(
        direction_kernel, [((384, count), BF16)], edges, geo, pool, at, lift, base, win, wout,
        flops=1_000_000_000,
    )

    dleft, down, dright, dh2, e2, drad, base2, da = call(
        second_kernel,
        [((288, 128), BF16), ((288, 128), F32), ((288, 128), BF16), ((32, 128), F32), ((8, 32), F32),
         ((384, count), BF16), ((384, count), BF16), ((288, 128), BF16)],
        left, own, right, hotref, rad, pool, wup, lam, w_mix, read_hidden, seed2,
    )

    plane = down + move(dleft, shift(2, 1)).astype(F32) + move(dright, shift(2, -1)).astype(F32)
    line = (
        plane[96:192]
        + move(plane[0:96].astype(BF16), shift(1, 1)).astype(F32)
        + move(plane[192:288].astype(BF16), shift(1, -1)).astype(F32)
    )
    folded = (
        line[32:64]
        + move(line[0:32].astype(BF16), shift(0, 1)).astype(F32)
        + move(line[64:96].astype(BF16), shift(0, -1)).astype(F32)
    )

    (drel2,) = call(
        slope_kernel, [((8, count), F32)], edges, geo, slope, drad, base2, da, woutb,
        flops=1_000_000_000,
    )

    left, own, right = pl.pallas_call(
        force_kernel,
        out_shape=tuple(jax.ShapeDtypeStruct((9, 128), F32) for _ in range(3)),
        scratch_shapes=[pltpu.VMEM((32, 128), F32)],
        compiler_params=pltpu.CompilerParams(vmem_limit_bytes=40 * 1024 * 1024),
        cost_estimate=pl.CostEstimate(flops=1_000_000, bytes_accessed=1_000_000, transcendentals=0),
    )(edges, folded, dh2, seed1, e1, e2, w_up, w_mix, v, drel2)

    plane = own + move(left, shift(2, 1)) + move(right, shift(2, -1))
    line = plane[3:6] + move(plane[0:3], shift(1, 1)) + move(plane[6:9], shift(1, -1))
    row = sum(move(line[d + 1 : d + 2], send_back(d)) for d in (-1, 0, 1))
    forces = row[0, : 3 * atoms].reshape(3, 1, 1, 1, atoms)
    site_energy = row[0, 3 * atoms :].reshape(1, 1, 1, atoms)
    return (site_energy, forces)


def solution(mesh):
    cell = P("gx", "gy", "gz")
    in_specs = (
        P(None, "gx", "gy", "gz", None),
        P("gx", "gy", "gz", None),
        cell,
        cell,
        P("gx", "gy", "gz", None),
        P("gx", "gy", "gz", None),
        P(None, "gx", "gy", "gz", None),
    ) + (P(),) * 9
    out_specs = (P("gx", "gy", "gz", None), P(None, "gx", "gy", "gz", None))
    return jax.shard_map(local, mesh=mesh, in_specs=in_specs, out_specs=out_specs, check_vma=False)
```

```python
import functools

import jax
import jax.numpy as jnp
import numpy as np
from jax import lax
from jax.experimental import pallas as pl
from jax.experimental.pallas import tpu as pltpu
from jax.sharding import PartitionSpec as P

cutoff_radius = 5.0
lattice_step = 2.25
AXES = ("gx", "gy", "gz")
SIDE = 8
F32 = jnp.float32
BF16 = jnp.bfloat16
S3 = 3.0**0.5
S5 = 5.0**0.5
S15 = 15.0**0.5
HIGH = lax.Precision.HIGHEST


def place(a, b, d):
    return (a * SIDE + b) * SIDE + d


def home(a, b, d):
    return place((a % 4) * 2 + d % 2, b, (d // 2) * 2 + a // 4)


def bricks():
    return [(a, b, d) for a in range(SIDE) for b in range(SIDE) for d in range(SIDE)]


def move(x, pairs):
    return lax.ppermute(x, AXES, pairs)


def bring_home():
    return [(place(a, b, d), home(a, b, d)) for a, b, d in bricks()]


def around():
    gx, gz = lax.axis_index("gx"), lax.axis_index("gz")
    a, d = (gz % 2) * 4 + gx // 2, (gz // 2) * 2 + gx % 2
    step = np.arange(-1, 2, dtype=np.int32)
    dz, dx = jnp.asarray(np.repeat(step, 3)), jnp.asarray(np.tile(step, 3))
    return ((a + dx) % SIDE) * SIDE + (d + dz) % SIDE


def exchange(x):
    return lax.all_to_all(x, ("gx", "gz"), 0, 0, tiled=True)


def shift(axis, step):
    pairs = []
    for cell in bricks():
        other = list(cell)
        other[axis] = (other[axis] + step) % SIDE
        pairs.append((home(*other), home(*cell)))
    return pairs


def widen(x, axis):
    return [move(x, shift(axis, -1)), x, move(x, shift(axis, 1))]


def nn(a, b, **kw):
    return lax.dot_general(a, b, (((1,), (0,)), ((), ())), preferred_element_type=F32, **kw)


def nt(a, b, **kw):
    return lax.dot_general(a, b, (((1,), (1,)), ((), ())), preferred_element_type=F32, **kw)


def tn(a, b, **kw):
    return lax.dot_general(a, b, (((0,), (0,)), ((), ())), preferred_element_type=F32, **kw)


def split(x):
    hi = x.astype(BF16)
    return hi, (x - hi.astype(F32)).astype(BF16)


def stack3(x):
    hi, lo = split(x)
    return jnp.concatenate([hi, lo, hi], axis=0)


def hot(index, rows):
    edges = index.shape[1]
    return lax.broadcasted_iota(jnp.int32, (rows, edges), 0) == index


def ones_at(index, rows):
    return jnp.where(hot(index, rows), 1.0, 0.0).astype(F32)


def small_stack(x):
    hi, lo = split(x)
    hi, lo = hi.astype(F32), lo.astype(F32)
    return jnp.concatenate([hi, lo, hi, jnp.zeros_like(x)], axis=0).astype(BF16)


def hidden_units(d2, env, denv, win):
    edges = d2.shape[1]
    centre = lax.broadcasted_iota(jnp.int32, (8, edges), 0).astype(F32) * (1.0 / 7.0)
    gap = d2 - centre
    basis = jnp.exp(-64.0 * gap * gap)
    slope = basis * (-128.0 * gap)
    pre = nn(win, small_stack(basis))
    dpre = nn(win, small_stack(slope))
    sig = 1.0 / (1.0 + jnp.exp(-pre))
    act = pre * sig
    dact = sig * (1.0 + pre * (1.0 - sig)) * dpre
    return act * env, dact * env + act * denv


def call(kernel, outs, *args, flops=1_000_000, limit=16, scratch=(), far=False, index=False):
    params = {}
    if index:
        params["in_specs"] = [pl.BlockSpec(memory_space=pltpu.SMEM)] + [
            pl.BlockSpec(memory_space=pltpu.VMEM)
        ] * (len(args) - 1)
    if far:
        spaces = [pltpu.SMEM if a.size == 1 else pltpu.HBM for a in args]
        args = [
            a if s is pltpu.SMEM else pltpu.with_memory_space_constraint(a, s)
            for a, s in zip(args, spaces)
        ]
        params["in_specs"] = [pl.BlockSpec(memory_space=s) for s in spaces]
        scratch = list(scratch) + [pltpu.SemaphoreType.DMA((len(args),))]
    return pl.pallas_call(
        kernel,
        out_shape=tuple(jax.ShapeDtypeStruct(s, d) for s, d in outs),
        scratch_shapes=scratch,
        compiler_params=pltpu.CompilerParams(vmem_limit_bytes=limit * 1024 * 1024),
        cost_estimate=pl.CostEstimate(flops=flops, bytes_accessed=1_000_000, transcendentals=0),
        **params,
    )(*args)


def fetch(sources, targets, sems):
    copies = [
        pltpu.make_async_copy(s, t, sems.at[i]) for i, (s, t) in enumerate(zip(sources, targets))
    ]
    for copy in copies:
        copy.start()
    for copy in copies:
        copy.wait()


def like(*args):
    return [pltpu.VMEM(a.shape, a.dtype) for a in args]


def pack_kernel(*refs):
    (atom_count, edge_count), far, (rows_o, edges_o) = refs[:2], refs[2:6], refs[6:8]
    near, sems = refs[8:12], refs[12]
    fetch(far, near, sems)
    positions, species, sender, receiver = near
    atoms, count = species.shape[-1], sender.shape[-1]
    owned = lax.broadcasted_iota(jnp.int32, (1, atoms), 1) < atom_count[0, 0, 0]
    kinds = jnp.where(owned, species[0, 0], -1).astype(F32)
    for c, part in enumerate([positions[k, 0, 0] for k in range(3)] + [kinds]):
        rows_o[0, :, atoms * c : atoms * c + atoms] = part
    rows_o[1:] = jnp.broadcast_to(rows_o[0:1], (rows_o.shape[0] - 1, 1, 4 * atoms))
    live = lax.broadcasted_iota(jnp.int32, (1, count), 1) < edge_count[0, 0, 0]
    s, r = sender[0, 0], receiver[0, 0]
    block, slot = jnp.right_shift(s, 5), jnp.bitwise_and(s, 31)
    one = lambda flag: jnp.where(flag, 1, 0)
    bx = one(block >= 9) + one(block >= 18)
    block = block - 9 * bx
    by = one(block >= 3) + one(block >= 6)
    bz = block - 3 * by
    s = (bz * 9 + by * 3 + bx) * 32 + slot
    edges_o[0:1] = jnp.where(live, s, 1023)
    edges_o[1:2] = jnp.where(live, r, 99)


def weights_kernel(*refs):
    far, outs, near, sems = refs[:9], refs[9:21], refs[21:25], refs[25]
    emb_o, t0_o, win_o, wout_o, woutb_o, wup_o, wupt_o, lam_o, wmix_o, one_o, hidden_o, out_o = outs
    fetch(far, list(near) + [lam_o, wmix_o, one_o, hidden_o, out_o], sems)
    embed, rin, rout, wup = near
    wupt_o[...] = wup[1]
    emb_o[...] = jnp.zeros_like(emb_o)
    emb_o[0 : embed.shape[0]] = embed[...].astype(BF16).astype(F32)
    table = nn(emb_o[...], wup[0], precision=HIGH)
    hi, lo = split(table.T)
    t0_o[...] = jnp.concatenate([hi, lo], axis=1)
    for t in range(2):
        hi, lo = split(rin[t])
        hi, lo = hi.astype(F32), lo.astype(F32)
        both = jnp.concatenate([hi, hi, lo, jnp.zeros_like(hi)], axis=0)
        win_o[t] = both.T.astype(BF16)
        hi, lo = split(rout[t])
        woutb_o[t] = hi
        hi, lo = hi.astype(F32), lo.astype(F32)
        both = jnp.concatenate([hi, hi, lo], axis=0)
        wout_o[t] = both.T.astype(BF16)
    hi, lo = split(wup[1].T)
    wup_o[...] = jnp.concatenate([hi, lo], axis=1)


def first_kernel(
    box, places, below, level, above, edges, emb, t0, win, wout, lam, wmix, read_one, read_out,
    h1_o, e1_o, seed1_o, seed2_o, geo_o, pool_o, at_o, lift_o, base_o, table,
):
    table[...] = jnp.zeros_like(table)
    for k in range(9):
        for dy, plane in enumerate((below, level, above)):
            at = k // 3 * 9 + dy * 3 + k % 3
            table[at : at + 1] = plane[places[k]]
    rows = table[...]
    hi = rows.astype(BF16).astype(F32)
    rest = rows - hi
    mid = rest.astype(BF16).astype(F32)
    low = rest - mid
    parts = [
        jnp.concatenate([p[:, 32 * c : 32 * c + 32] for p in (hi, mid, low)], axis=1)
        for c in range(4)
    ]
    lhs = jnp.concatenate(parts, axis=0).astype(BF16)
    mine = jnp.concatenate([p[13:14] for p in parts] + [jnp.zeros((4, 96), F32)], axis=0)
    sender = edges[0:1]
    receiver = edges[1:2]
    slot = ones_at(jnp.bitwise_and(sender, 31), 32).astype(BF16)
    block = ones_at(jnp.right_shift(sender, 5), 32)
    recv = ones_at(receiver, 32)
    recv_b = recv.astype(BF16)
    got = nn(lhs, jnp.concatenate([slot] * 3, axis=0))
    at_recv = nn(mine.astype(BF16), jnp.concatenate([recv_b] * 3, axis=0))
    sent = [jnp.sum(got[32 * c : 32 * c + 32] * block, axis=0, keepdims=True) for c in range(4)]
    rel = []
    for c in range(3):
        d = sent[c] - at_recv[c : c + 1]
        d = d - jnp.round(d * (1.0 / box[c])) * box[c]
        rel.append(d * (1.0 / cutoff_radius))
    x, y, z = rel
    d2 = x * x + y * y + z * z
    reach = jnp.maximum(1.0 - d2, 0.0)
    env = reach * reach
    denv = -2.0 * reach
    geo_o[...] = jnp.concatenate([x, y, z, d2, env, denv, d2, d2], axis=0)
    harmonics = [
        jnp.ones_like(x),
        S3 * x,
        S3 * y,
        S3 * z,
        S15 * x * y,
        S15 * y * z,
        S15 * x * z,
        0.5 * S15 * (x * x - y * y),
        0.5 * S5 * (2.0 * z * z - x * x - y * y),
    ]
    for m, value in enumerate(harmonics):
        pool_o[32 * m : 32 * m + 32] = (recv * (value * 0.125)).astype(BF16)
    hidden, _ = hidden_units(d2, env, denv, win[0])
    radial = nn(wout[0], stack3(hidden))
    kind = ones_at(sent[3].astype(jnp.int32), 128).astype(BF16)
    lift = nn(t0[...], jnp.concatenate([kind, kind], axis=0))
    lift_o[...] = lift.astype(BF16)
    sums = []
    for order, (a, b) in enumerate(((0, 32), (32, 128), (128, 288))):
        base = (radial[128 * order : 128 * order + 128] * lift).astype(BF16)
        base_o[128 * order : 128 * order + 128] = base
        sums.append(nt(pool_o[a:b], base))
    product = sums[0]
    for order in (1, 2):
        total = sums[order]
        weight = lam[0, order - 1 : order]
        square = sum(
            total[32 * m : 32 * m + 32] * total[32 * m : 32 * m + 32]
            for m in range(2 * order + 1)
        )
        product = product + weight * square
        first = 0 if order == 1 else 96
        at_o[first : first + 32 * (2 * order + 1)] = (2.0 * weight * total).astype(BF16)
    kinds = rows[13:14, 96:128]
    mask = jnp.where(kinds >= 0.0, 1.0, 0.0)
    own_kind = jnp.where(
        lax.broadcasted_iota(jnp.int32, (128, 32), 0) == kinds.astype(jnp.int32), 1.0, 0.0
    ).astype(BF16)
    h0 = tn(own_kind, emb[...].astype(BF16))
    h1 = h0 + nn(product, wmix[0], precision=HIGH)
    h1_o[...] = h1.astype(BF16)
    e1_o[...] = nt(read_one[...], h1, precision=HIGH) * mask
    pad = jnp.zeros((7, 32), F32)
    mask8 = jnp.concatenate([mask, pad], axis=0)
    zero = lax.broadcasted_iota(jnp.int32, (8, 128), 0) == 0
    seed1_o[...] = tn(mask8, jnp.where(zero, read_one[...], 0.0), precision=HIGH)
    zero = lax.broadcasted_iota(jnp.int32, (8, 16), 0) == 0
    seed2_o[...] = tn(mask8, jnp.where(zero, read_out[...], 0.0), precision=HIGH)


def radial_kernel(edges, geo, win, wout, hot_o, rad_o, slope_o):
    sender = edges[0:1]
    for r in range(0, 864, 96):
        row = lax.broadcasted_iota(jnp.int32, (96, sender.shape[1]), 0) + r
        hot_o[r : r + 96] = jnp.where(row == sender, 1.0, 0.0).astype(BF16)
    hidden, slope = hidden_units(geo[3:4], geo[4:5], geo[5:6], win[1])
    rad_o[...] = nn(wout[1], stack3(hidden))
    slope_o[...] = slope


def direction_kernel(edges, geo, pool, at, lift, base, win, wout, v_o):
    x, y, z = geo[0:1], geo[1:2], geo[2:3]
    recv = ones_at(edges[1:2], 32)
    _, slope = hidden_units(geo[3:4], geo[4:5], geo[5:6], win[0])
    drad = nn(wout[0], stack3(slope))
    g1 = tn(at[0:96], pool[32:128])
    g2 = tn(at[96:256], pool[128:288])
    common = drad[0:128] * 0.125 + drad[128:256] * g1 + drad[256:384] * g2
    common = lift[...].astype(F32) * common
    b1 = base[128:256].astype(F32)
    b2 = base[256:384].astype(F32)
    recv8 = recv * 0.125
    turns = (
        ((0, S15 * y), (2, S15 * z), (3, S15 * x), (4, -S5 * x)),
        ((0, S15 * x), (1, S15 * z), (3, -S15 * y), (4, -S5 * y)),
        ((1, S15 * y), (2, S15 * x), (4, 2.0 * S5 * z)),
    )
    for k, coordinate in enumerate((x, y, z)):
        h1 = tn(at[32 * k : 32 * k + 32], (recv8 * S3).astype(BF16))
        left = jnp.concatenate([at[96 + 32 * m : 128 + 32 * m] for m, _ in turns[k]], axis=0)
        right = jnp.concatenate([(recv8 * f).astype(BF16) for _, f in turns[k]], axis=0)
        h2 = tn(left, right)
        v = common * (2.0 * coordinate) + b1 * h1 + b2 * h2
        v_o[128 * k : 128 * k + 128] = v.astype(BF16)


def second_kernel(
    left, own, right, hotref, rad, pool, wup, lam, wmix, read_hidden, seed2,
    dleft_o, down_o, dright_o, dh2_o, e2_o, drad_o, base_o, da_o,
):
    feats = jnp.concatenate([left[...], own[...], right[...]], axis=0)
    got = tn(feats, hotref[...]).astype(BF16)
    lift = nn(wup[...], jnp.concatenate([got, got], axis=0))
    sums = []
    spans = ((0, 32), (32, 128), (128, 288))
    for order, (a, b) in enumerate(spans):
        base = (rad[128 * order : 128 * order + 128] * lift).astype(BF16)
        base_o[128 * order : 128 * order + 128] = base
        sums.append(nt(pool[a:b], base))
    product = sums[0]
    for order in (1, 2):
        total = sums[order]
        square = sum(
            total[32 * m : 32 * m + 32] * total[32 * m : 32 * m + 32]
            for m in range(2 * order + 1)
        )
        product = product + lam[1, order - 1 : order] * square
    h2 = own[128:160].astype(F32) + nn(product, wmix[1], precision=HIGH)
    pre = nt(h2, read_hidden[...], precision=HIGH)
    sig = 1.0 / (1.0 + jnp.exp(-pre))
    inner = pre * sig
    seed = seed2[...]
    e2_o[...] = nt(jnp.ones((8, 16), F32), inner * seed, precision=HIGH)
    dpre = seed * sig * (1.0 + pre * (1.0 - sig))
    dh2 = nn(dpre, read_hidden[...], precision=HIGH)
    dh2_o[...] = dh2
    dp = nt(dh2, wmix[1], precision=HIGH)
    da_o[0:32] = dp.astype(BF16)
    for order in (1, 2):
        weight = 2.0 * lam[1, order - 1 : order] * dp
        a = spans[order][0]
        for m in range(2 * order + 1):
            piece = weight * sums[order][32 * m : 32 * m + 32]
            da_o[a + 32 * m : a + 32 * m + 32] = piece.astype(BF16)
    dlift = None
    for order, (a, b) in enumerate(spans):
        g = tn(da_o[a:b], pool[a:b])
        drad_o[128 * order : 128 * order + 128] = (lift * g).astype(BF16)
        term = rad[128 * order : 128 * order + 128] * g
        dlift = term if dlift is None else dlift + term
    hi, lo = split(dlift)
    back = nt(hotref[...], jnp.concatenate([hi, lo], axis=0))
    back = back[:, 0:128] + back[:, 128:256]
    dleft_o[...] = back[0:288].astype(BF16)
    down_o[...] = back[288:576]
    dright_o[...] = back[576:864].astype(BF16)


def slope_kernel(edges, geo, slope, drad, base, da, woutb, drel_o):
    x, y, z = geo[0:1], geo[1:2], geo[2:3]
    recv8 = ones_at(edges[1:2], 32) * 0.125
    dhidden = nn(woutb[1], drad[...])
    dd2 = 2.0 * jnp.sum(dhidden * slope[...], axis=0, keepdims=True)
    q1 = nn(da[32:128], base[128:256])
    q2 = nn(da[128:288], base[256:384])
    one = [
        jnp.sum(q1[32 * m : 32 * m + 32] * recv8, axis=0, keepdims=True) * S3 for m in range(3)
    ]
    two = [jnp.sum(q2[32 * m : 32 * m + 32] * recv8, axis=0, keepdims=True) for m in range(5)]
    dx = dd2 * x + one[0] + S15 * (two[0] * y + two[2] * z + two[3] * x) - S5 * two[4] * x
    dy = dd2 * y + one[1] + S15 * (two[0] * x + two[1] * z - two[3] * y) - S5 * two[4] * y
    dz = dd2 * z + one[2] + S15 * (two[1] * y + two[2] * x) + 2.0 * S5 * two[4] * z
    none = jnp.zeros_like(dx)
    drel_o[...] = jnp.concatenate([dx, dy, dz, none, none, none, none, none], axis=0)


def force_kernel(edges, folded, dh2, seed1, e1, e2, wup, wmix, v, drel2, below_o, level_o, above_o, rows):
    dh1 = dh2[...] + seed1[...] + nt(folded[...], wup[...], precision=HIGH)
    dp = nt(dh1, wmix[0], precision=HIGH)
    hi, lo = split(dp)
    dp2 = jnp.concatenate([hi, lo], axis=0)
    sender = edges[0:1]
    recv = ones_at(edges[1:2], 32)
    slot = ones_at(jnp.bitwise_and(sender, 31), 32).astype(BF16)
    block = ones_at(jnp.right_shift(sender, 5), 32)
    spread, pulled = [], []
    for k in range(3):
        q = nn(dp2, v[128 * k : 128 * k + 128])
        q = q[0:32] + q[32:64]
        drel = jnp.sum(q * recv, axis=0, keepdims=True) + drel2[k : k + 1]
        force = drel * (-1.0 / cutoff_radius)
        hi, lo = split(force)
        hi, lo = hi.astype(F32), lo.astype(F32)
        spread += [block * hi, block * lo]
        pulled += [hi, lo]
    pushed = nt(jnp.concatenate(spread, axis=0).astype(BF16), slot)
    pulled = jnp.concatenate(pulled + [jnp.zeros_like(hi)] * 2, axis=0).astype(BF16)
    pulled = nt(pulled, recv.astype(BF16))
    rows[...] = jnp.zeros_like(rows)
    for k in range(3):
        rows[:, 32 * k : 32 * k + 32] = pushed[64 * k : 64 * k + 32] + pushed[64 * k + 32 : 64 * k + 64]
        rows[13:14, 32 * k : 32 * k + 32] = (
            rows[13:14, 32 * k : 32 * k + 32] - pulled[2 * k : 2 * k + 1] - pulled[2 * k + 1 : 2 * k + 2]
        )
    rows[13:14, 96:128] = e1[...] + e2[0:1]
    for dz in range(3):
        for dy, out in enumerate((below_o, level_o, above_o)):
            out[3 * dz : 3 * dz + 3] = rows[9 * dz + 3 * dy : 9 * dz + 3 * dy + 3]


def spread_kernel(places, a, b, c, out):
    out[...] = jnp.zeros_like(out)
    total = a[...] + b[...] + c[...]
    for k in range(9):
        out[places[k]] = total[k : k + 1]


def last_kernel(rows, energy_o, forces_o):
    atoms = energy_o.shape[-1]
    total = jnp.sum(rows[...], axis=0)
    energy_o[0, 0] = total[:, 3 * atoms : 4 * atoms]
    for k in range(3):
        forces_o[k, 0, 0] = total[:, atoms * k : atoms * k + atoms]


def local(
    positions, species, atom_count, edge_count, sender, receiver, image_shift,
    embed, radial_in, radial_out, w_up, lam, w_mix, read_one, read_hidden, read_out,
):
    atoms = positions.shape[-1]
    count = sender.shape[-1]
    box = (SIDE * 4 * lattice_step, SIDE * 4 * lattice_step, SIDE * (atoms // 16) * lattice_step)

    places = around()
    rows, edges = call(
        pack_kernel, [((SIDE * SIDE, 1, 4 * atoms), F32), ((2, count), jnp.int32)],
        atom_count, edge_count, positions, species, sender, receiver, far=True,
        scratch=like(positions, species, sender, receiver),
    )
    level = exchange(rows)
    below, level, above = widen(level, 1)
    edges = move(edges, bring_home())

    weights = call(
        weights_kernel,
        [((128, 128), F32), ((128, 256), BF16), ((2, 64, 32), BF16), ((2, 384, 192), BF16),
         ((2, 64, 384), BF16), ((128, 256), BF16), ((128, 128), F32), ((2, 2, 128), F32), ((2, 128, 128), F32),
         ((1, 128), F32), ((16, 128), F32), ((1, 16), F32)],
        embed, radial_in, radial_out, w_up, lam, w_mix, read_one[None], read_hidden.T, read_out[None],
        far=True, scratch=like(embed, radial_in, radial_out, w_up),
    )
    emb, t0, win, wout, woutb, wup, wup_t, lam, w_mix, read_one, read_hidden, read_out = weights

    h1, e1, seed1, seed2, geo, pool, at, lift, base = call(
        functools.partial(first_kernel, box),
        [((32, 128), BF16), ((1, 32), F32), ((32, 128), F32), ((32, 16), F32), ((8, count), F32),
         ((288, count), BF16), ((256, 128), BF16), ((128, count), BF16), ((384, count), BF16)],
        places, below, level, above, edges, emb, t0, win, wout, lam, w_mix, read_one, read_out,
        scratch=[pltpu.VMEM((32, 128), F32)], index=True,
    )

    line = jnp.concatenate(widen(h1, 0), axis=0)
    hidden = call(
        radial_kernel,
        [((864, count), BF16), ((384, count), F32), ((64, count), F32)],
        edges, geo, win, wout, flops=1_000_000_000,
    )
    line, (hotref, rad, slope) = lax.optimization_barrier((line, hidden))
    plane = jnp.concatenate(widen(line, 1), axis=0)
    hidden = call(
        direction_kernel, [((384, count), BF16)], edges, geo, pool, at, lift, base, win, wout,
        flops=1_000_000_000,
    )
    plane, (v,) = lax.optimization_barrier((plane, hidden))
    left, own, right = widen(plane, 2)

    dleft, down, dright, dh2, e2, drad, base2, da = call(
        second_kernel,
        [((288, 128), BF16), ((288, 128), F32), ((288, 128), BF16), ((32, 128), F32), ((8, 32), F32),
         ((384, count), BF16), ((384, count), BF16), ((288, 128), BF16)],
        left, own, right, hotref, rad, pool, wup, lam, w_mix, read_hidden, seed2,
    )

    plane = down + move(dleft, shift(2, 1)).astype(F32) + move(dright, shift(2, -1)).astype(F32)
    line = (
        plane[96:192]
        + move(plane[0:96].astype(BF16), shift(1, 1)).astype(F32)
        + move(plane[192:288].astype(BF16), shift(1, -1)).astype(F32)
    )
    folded = (
        line[32:64]
        + move(line[0:32].astype(BF16), shift(0, 1)).astype(F32)
        + move(line[64:96].astype(BF16), shift(0, -1)).astype(F32)
    )

    (drel2,) = call(
        slope_kernel, [((8, count), F32)], edges, geo, slope, drad, base2, da, woutb,
        flops=1_000_000_000,
    )

    below, level, above = call(
        force_kernel, [((9, 128), F32)] * 3,
        edges, folded, dh2, seed1, e1, e2, wup_t, w_mix, v, drel2,
        scratch=[pltpu.VMEM((32, 128), F32)],
    )

    (rows,) = call(
        spread_kernel, [((SIDE * SIDE, 1, 4 * atoms), F32)],
        places, level, move(below, shift(1, 1)), move(above, shift(1, -1)), index=True,
    )
    return call(
        last_kernel, [((1, 1, 1, atoms), F32), ((3, 1, 1, 1, atoms), F32)], exchange(rows)
    )


def solution(mesh):
    cell = P("gx", "gy", "gz")
    in_specs = (
        P(None, "gx", "gy", "gz", None),
        P("gx", "gy", "gz", None),
        cell,
        cell,
        P("gx", "gy", "gz", None),
        P("gx", "gy", "gz", None),
        P(None, "gx", "gy", "gz", None),
    ) + (P(),) * 9
    out_specs = (P("gx", "gy", "gz", None), P(None, "gx", "gy", "gz", None))
    return jax.shard_map(local, mesh=mesh, in_specs=in_specs, out_specs=out_specs, check_vma=False)
```

```python
import functools

import jax
import jax.numpy as jnp
import numpy as np
from jax import lax
from jax.experimental import pallas as pl
from jax.experimental.pallas import tpu as pltpu
from jax.sharding import PartitionSpec as P

cutoff_radius = 5.0
lattice_step = 2.25
AXES = ("gx", "gy", "gz")
SIDE = 8
F32 = jnp.float32
BF16 = jnp.bfloat16
S3 = 3.0**0.5
S5 = 5.0**0.5
S15 = 15.0**0.5
HIGH = lax.Precision.HIGHEST


def place(a, b, d):
    return (a * SIDE + b) * SIDE + d


def home(a, b, d):
    return place((a % 4) * 2 + d % 2, b, (d // 2) * 2 + a // 4)


def bricks():
    return [(a, b, d) for a in range(SIDE) for b in range(SIDE) for d in range(SIDE)]


def move(x, pairs):
    return lax.ppermute(x, AXES, pairs)


def bring_home():
    return [(place(a, b, d), home(a, b, d)) for a, b, d in bricks()]


def here():
    gx, gz = lax.axis_index("gx"), lax.axis_index("gz")
    return jnp.stack([(gz % 2) * 4 + gx // 2, (gz // 2) * 2 + gx % 2])


def around(brick, k):
    a, d = brick[0] + (k // 3 - 2 + SIDE), brick[1] + (k % 3 - 1 + SIDE)
    return jnp.bitwise_and(a, SIDE - 1) * SIDE + jnp.bitwise_and(d, SIDE - 1)


def exchange(x):
    rows = x.reshape(x.shape[0], 1, x.shape[1])
    return lax.all_to_all(rows, ("gx", "gz"), 0, 0, tiled=True).reshape(x.shape)


def shift(axis, step):
    pairs = []
    for cell in bricks():
        other = list(cell)
        other[axis] = (other[axis] + step) % SIDE
        pairs.append((home(*other), home(*cell)))
    return pairs


def widen(x, axis):
    return [move(x, shift(axis, -1)), x, move(x, shift(axis, 1))]


def nn(a, b, **kw):
    return lax.dot_general(a, b, (((1,), (0,)), ((), ())), preferred_element_type=F32, **kw)


def nt(a, b, **kw):
    return lax.dot_general(a, b, (((1,), (1,)), ((), ())), preferred_element_type=F32, **kw)


def tn(a, b, **kw):
    return lax.dot_general(a, b, (((0,), (0,)), ((), ())), preferred_element_type=F32, **kw)


def split(x):
    hi = x.astype(BF16)
    return hi, (x - hi.astype(F32)).astype(BF16)


def stack3(x):
    hi, lo = split(x)
    return jnp.concatenate([hi, lo, hi], axis=0)


def product3(x, stack):
    hi, lo = split(x)
    return nn(jnp.concatenate([hi, lo, hi], axis=1), stack)


def rows3(w):
    hi, lo = split(w)
    return jnp.concatenate([hi, hi, lo], axis=0)


def hot(index, rows):
    edges = index.shape[1]
    return lax.broadcasted_iota(jnp.int32, (rows, edges), 0) == index


def ones_at(index, rows):
    return jnp.where(hot(index, rows), 1.0, 0.0).astype(F32)


def small_stack(x):
    hi, lo = split(x)
    hi, lo = hi.astype(F32), lo.astype(F32)
    return jnp.concatenate([hi, lo, hi, jnp.zeros_like(x)], axis=0).astype(BF16)


def hidden_units(d2, env, denv, win):
    edges = d2.shape[1]
    centre = lax.broadcasted_iota(jnp.int32, (8, edges), 0).astype(F32) * (1.0 / 7.0)
    gap = d2 - centre
    basis = jnp.exp(-64.0 * gap * gap)
    slope = basis * (-128.0 * gap)
    pre = nn(win, small_stack(basis))
    dpre = nn(win, small_stack(slope))
    sig = 1.0 / (1.0 + jnp.exp(-pre))
    act = pre * sig
    dact = sig * (1.0 + pre * (1.0 - sig)) * dpre
    return act * env, dact * env + act * denv


def call(kernel, outs, *args, flops=1_000_000, limit=16, scratch=(), far=False, index=False):
    params = {}
    if index:
        params["in_specs"] = [pl.BlockSpec(memory_space=pltpu.SMEM)] + [
            pl.BlockSpec(memory_space=pltpu.VMEM)
        ] * (len(args) - 1)
    if far:
        spaces = [pltpu.SMEM if a.size == 1 else pltpu.HBM for a in args]
        args = [
            a if s is pltpu.SMEM else pltpu.with_memory_space_constraint(a, s)
            for a, s in zip(args, spaces)
        ]
        params["in_specs"] = [pl.BlockSpec(memory_space=s) for s in spaces]
        scratch = list(scratch) + [pltpu.SemaphoreType.DMA((len(args),))]
    return pl.pallas_call(
        kernel,
        out_shape=tuple(jax.ShapeDtypeStruct(s, d) for s, d in outs),
        scratch_shapes=scratch,
        compiler_params=pltpu.CompilerParams(vmem_limit_bytes=limit * 1024 * 1024),
        cost_estimate=pl.CostEstimate(flops=flops, bytes_accessed=1_000_000, transcendentals=0),
        **params,
    )(*args)


def fetch(sources, targets, sems):
    copies = [
        pltpu.make_async_copy(s, t, sems.at[i]) for i, (s, t) in enumerate(zip(sources, targets))
    ]
    for copy in copies:
        copy.start()
    for copy in copies:
        copy.wait()


def like(*args):
    return [pltpu.VMEM(a.shape, a.dtype) for a in args]


def pack_kernel(*refs):
    (atom_count, edge_count), far, (rows_o, edges_o) = refs[:2], refs[2:6], refs[6:8]
    near, sems = refs[8:12], refs[12]
    fetch(far, near, sems)
    positions, species, sender, receiver = near
    atoms, count = species.shape[-1], sender.shape[-1]
    owned = lax.broadcasted_iota(jnp.int32, (1, atoms), 1) < atom_count[0, 0, 0]
    kinds = jnp.where(owned, species[0, 0], -1).astype(F32)
    for c, part in enumerate([positions[k, 0, 0] for k in range(3)] + [kinds]):
        rows_o[0:1, atoms * c : atoms * c + atoms] = part
    rows_o[...] = jnp.broadcast_to(rows_o[0:1], rows_o.shape)
    live = lax.broadcasted_iota(jnp.int32, (1, count), 1) < edge_count[0, 0, 0]
    s, r = sender[0, 0], receiver[0, 0]
    edges_o[0:1] = jnp.where(live, s, 1023)
    edges_o[1:2] = jnp.where(live, r, 99)


def weights_kernel(*refs):
    far, outs, near, sems = refs[:9], refs[9:23], refs[23:28], refs[28]
    (emb_o, t0_o, win_o, wout_o, woutb_o, wup_o, mix_o, mixt_o, wupt_o, hw_o), kept = outs[:10], outs[10:]
    fetch(far, list(near) + list(kept), sems)
    embed, rin, rout, wup, wmix = near
    wupt_o[...] = rows3(wup[1].T)
    for t in range(2):
        mix_o[t] = rows3(wmix[t])
        mixt_o[t] = rows3(wmix[t].T)
    hw_o[...] = rows3(kept[2][...].T)
    emb_o[...] = jnp.zeros_like(emb_o)
    emb_o[0 : embed.shape[0]] = embed[...].astype(BF16).astype(F32)
    table = nn(emb_o[...], wup[0], precision=HIGH)
    hi, lo = split(table.T)
    t0_o[...] = jnp.concatenate([hi, lo], axis=1)
    for t in range(2):
        hi, lo = split(rin[t])
        hi, lo = hi.astype(F32), lo.astype(F32)
        both = jnp.concatenate([hi, hi, lo, jnp.zeros_like(hi)], axis=0)
        win_o[t] = both.T.astype(BF16)
        hi, lo = split(rout[t])
        woutb_o[t] = hi
        hi, lo = hi.astype(F32), lo.astype(F32)
        both = jnp.concatenate([hi, hi, lo], axis=0)
        wout_o[t] = both.T.astype(BF16)
    hi, lo = split(wup[1].T)
    wup_o[...] = jnp.concatenate([hi, lo], axis=1)


def own_kernel(box, *refs):
    (brick, below, level, above, edges), weights = refs[:5], refs[5:13]
    (e1_o, seed1_o, seed2_o, h1_o, parts, table), results = refs[13:19], refs[19:24]
    read_one, read_out = weights[6:]
    table[...] = jnp.zeros_like(table)
    for k in range(15):
        at = pl.ds(around(brick, k), 1)
        for dy, plane in enumerate((below, level, above)):
            row = k // 3 * 9 + dy * 3 + k % 3
            table[row : row + 1] = plane[at]
    rows = table[...]
    hi = rows.astype(BF16).astype(F32)
    rest = rows - hi
    mid = rest.astype(BF16).astype(F32)
    low = rest - mid
    for c in range(4):
        parts[c] = jnp.concatenate([p[:, 32 * c : 32 * c + 32] for p in (hi, mid, low)], axis=1)
    h1, mask = first_layer(box, 9, edges, *weights[:6], *results, table, parts)
    h1_o[...] = h1.astype(BF16)
    e1_o[...] = nt(read_one[...], h1, precision=HIGH) * mask
    mask8 = jnp.concatenate([mask, jnp.zeros((7, 32), F32)], axis=0)
    zero = lax.broadcasted_iota(jnp.int32, (8, 128), 0) == 0
    seed1_o[...] = tn(mask8, jnp.where(zero, read_one[...], 0.0), precision=HIGH)
    zero = lax.broadcasted_iota(jnp.int32, (8, 16), 0) == 0
    seed2_o[...] = tn(mask8, jnp.where(zero, read_out[...], 0.0), precision=HIGH)


def sides_kernel(box, before, after, parts, table, h1, *refs):
    weights, h1_o, results = refs[:6], refs[6], refs[7:]
    h1_o[32:64] = h1[...]
    for brick, edges in ((0, before), (2, after)):
        found = results[:5] if brick == 0 else results[5:]
        value, _ = first_layer(box, 9 * brick, edges, *weights, *found, table, parts)
        h1_o[32 * brick : 32 * brick + 32] = value.astype(BF16)


def first_layer(
    box, start, edges, emb, t0, win, wout, lam, mix, geo_o, pool_o, at_o, lift_o, base_o, table, parts
):
    lhs = jnp.concatenate([parts[c, start : start + 32] for c in range(4)], axis=0).astype(BF16)
    middle = start + 13
    mine = [parts[c, middle : middle + 1] for c in range(4)] + [jnp.zeros((4, 96), F32)]
    mine = jnp.concatenate(mine, axis=0)
    sender = edges[0:1]
    receiver = edges[1:2]
    slot = ones_at(jnp.bitwise_and(sender, 31), 32).astype(BF16)
    block = ones_at(jnp.right_shift(sender, 5), 32)
    recv = ones_at(receiver, 32)
    recv_b = recv.astype(BF16)
    got = nn(lhs, jnp.concatenate([slot] * 3, axis=0))
    at_recv = nn(mine.astype(BF16), jnp.concatenate([recv_b] * 3, axis=0))
    sent = [jnp.sum(got[32 * c : 32 * c + 32] * block, axis=0, keepdims=True) for c in range(4)]
    rel = []
    for c in range(3):
        d = sent[c] - at_recv[c : c + 1]
        d = d - jnp.round(d * (1.0 / box[c])) * box[c]
        rel.append(d * (1.0 / cutoff_radius))
    x, y, z = rel
    d2 = x * x + y * y + z * z
    reach = jnp.maximum(1.0 - d2, 0.0)
    env = reach * reach
    denv = -2.0 * reach
    geo_o[...] = jnp.concatenate([x, y, z, d2, env, denv, d2, d2], axis=0)
    harmonics = [
        jnp.ones_like(x),
        S3 * x,
        S3 * y,
        S3 * z,
        S15 * x * y,
        S15 * y * z,
        S15 * x * z,
        0.5 * S15 * (x * x - y * y),
        0.5 * S5 * (2.0 * z * z - x * x - y * y),
    ]
    for m, value in enumerate(harmonics):
        pool_o[32 * m : 32 * m + 32] = (recv * (value * 0.125)).astype(BF16)
    hidden, _ = hidden_units(d2, env, denv, win[0])
    radial = nn(wout[0], stack3(hidden))
    kind = ones_at(sent[3].astype(jnp.int32), 128).astype(BF16)
    lift = nn(t0[...], jnp.concatenate([kind, kind], axis=0))
    lift_o[...] = lift.astype(BF16)
    sums = []
    for order, (a, b) in enumerate(((0, 32), (32, 128), (128, 288))):
        base = (radial[128 * order : 128 * order + 128] * lift).astype(BF16)
        base_o[128 * order : 128 * order + 128] = base
        sums.append(nt(pool_o[a:b], base))
    product = sums[0]
    for order in (1, 2):
        total = sums[order]
        weight = lam[0, order - 1 : order]
        square = sum(
            total[32 * m : 32 * m + 32] * total[32 * m : 32 * m + 32]
            for m in range(2 * order + 1)
        )
        product = product + weight * square
        first = 0 if order == 1 else 96
        at_o[first : first + 32 * (2 * order + 1)] = (2.0 * weight * total).astype(BF16)
    kinds = table[middle : middle + 1, 96:128]
    mask = jnp.where(kinds >= 0.0, 1.0, 0.0)
    own_kind = jnp.where(
        lax.broadcasted_iota(jnp.int32, (128, 32), 0) == kinds.astype(jnp.int32), 1.0, 0.0
    ).astype(BF16)
    h0 = tn(own_kind, emb[...].astype(BF16))
    return h0 + product3(product, mix[0]), mask


def radial_kernel(edges, geo, win, wout, hot_o, rad_o, slope_o):
    s = edges[0:1]
    block, slot = jnp.right_shift(s, 5), jnp.bitwise_and(s, 31)
    one = lambda flag: jnp.where(flag, 1, 0)
    bx = one(block >= 9) + one(block >= 18)
    block = block - 9 * bx
    by = one(block >= 3) + one(block >= 6)
    bz = block - 3 * by
    s = (bz * 9 + by * 3 + bx) * 32 + slot
    sender = s
    for r in range(0, 864, 96):
        row = lax.broadcasted_iota(jnp.int32, (96, sender.shape[1]), 0) + r
        hot_o[r : r + 96] = jnp.where(row == sender, 1.0, 0.0).astype(BF16)
    hidden, slope = hidden_units(geo[3:4], geo[4:5], geo[5:6], win[1])
    rad_o[...] = nn(wout[1], stack3(hidden))
    slope_o[...] = slope


def direction_kernel(edges, geo, pool, at, lift, base, win, wout, v_o):
    x, y, z = geo[0:1], geo[1:2], geo[2:3]
    recv = ones_at(edges[1:2], 32)
    _, slope = hidden_units(geo[3:4], geo[4:5], geo[5:6], win[0])
    drad = nn(wout[0], stack3(slope))
    g1 = tn(at[0:96], pool[32:128])
    g2 = tn(at[96:256], pool[128:288])
    common = drad[0:128] * 0.125 + drad[128:256] * g1 + drad[256:384] * g2
    common = lift[...].astype(F32) * common
    b1 = base[128:256].astype(F32)
    b2 = base[256:384].astype(F32)
    recv8 = recv * 0.125
    turns = (
        ((0, S15 * y), (2, S15 * z), (3, S15 * x), (4, -S5 * x)),
        ((0, S15 * x), (1, S15 * z), (3, -S15 * y), (4, -S5 * y)),
        ((1, S15 * y), (2, S15 * x), (4, 2.0 * S5 * z)),
    )
    for k, coordinate in enumerate((x, y, z)):
        h1 = tn(at[32 * k : 32 * k + 32], (recv8 * S3).astype(BF16))
        left = jnp.concatenate([at[96 + 32 * m : 128 + 32 * m] for m, _ in turns[k]], axis=0)
        right = jnp.concatenate([(recv8 * f).astype(BF16) for _, f in turns[k]], axis=0)
        h2 = tn(left, right)
        v = common * (2.0 * coordinate) + b1 * h1 + b2 * h2
        v_o[128 * k : 128 * k + 128] = v.astype(BF16)


def second_kernel(
    left, own, right, hotref, rad, pool, wup, lam, mix, mix_t, hidden_w, read_hidden, seed2,
    dleft_o, down_o, dright_o, dh2_o, e2_o, drad_o, base_o, da_o,
):
    feats = jnp.concatenate([left[...], own[...], right[...]], axis=0)
    got = tn(feats, hotref[...]).astype(BF16)
    lift = nn(wup[...], jnp.concatenate([got, got], axis=0))
    sums = []
    spans = ((0, 32), (32, 128), (128, 288))
    for order, (a, b) in enumerate(spans):
        base = (rad[128 * order : 128 * order + 128] * lift).astype(BF16)
        base_o[128 * order : 128 * order + 128] = base
        sums.append(nt(pool[a:b], base))
    product = sums[0]
    for order in (1, 2):
        total = sums[order]
        square = sum(
            total[32 * m : 32 * m + 32] * total[32 * m : 32 * m + 32]
            for m in range(2 * order + 1)
        )
        product = product + lam[1, order - 1 : order] * square
    h2 = own[128:160].astype(F32) + product3(product, mix[1])
    pre = product3(h2, hidden_w[...])
    sig = 1.0 / (1.0 + jnp.exp(-pre))
    inner = pre * sig
    seed = seed2[...]
    e2_o[...] = nt(jnp.ones((8, 16), F32), inner * seed, precision=HIGH)
    dpre = seed * sig * (1.0 + pre * (1.0 - sig))
    dh2 = nn(dpre, read_hidden[...], precision=HIGH)
    dh2_o[...] = dh2
    dp = product3(dh2, mix_t[1])
    da_o[0:32] = dp.astype(BF16)
    for order in (1, 2):
        weight = 2.0 * lam[1, order - 1 : order] * dp
        a = spans[order][0]
        for m in range(2 * order + 1):
            piece = weight * sums[order][32 * m : 32 * m + 32]
            da_o[a + 32 * m : a + 32 * m + 32] = piece.astype(BF16)
    dlift = None
    for order, (a, b) in enumerate(spans):
        g = tn(da_o[a:b], pool[a:b])
        drad_o[128 * order : 128 * order + 128] = (lift * g).astype(BF16)
        term = rad[128 * order : 128 * order + 128] * g
        dlift = term if dlift is None else dlift + term
    hi, lo = split(dlift)
    back = nt(hotref[...], jnp.concatenate([hi, lo], axis=0))
    back = back[:, 0:128] + back[:, 128:256]
    dleft_o[...] = back[0:288].astype(BF16)
    down_o[...] = back[288:576]
    dright_o[...] = back[576:864].astype(BF16)


def slope_kernel(edges, geo, slope, drad, base, da, woutb, drel_o):
    x, y, z = geo[0:1], geo[1:2], geo[2:3]
    recv8 = ones_at(edges[1:2], 32) * 0.125
    dhidden = nn(woutb[1], drad[...])
    dd2 = 2.0 * jnp.sum(dhidden * slope[...], axis=0, keepdims=True)
    q1 = nn(da[32:128], base[128:256])
    q2 = nn(da[128:288], base[256:384])
    one = [
        jnp.sum(q1[32 * m : 32 * m + 32] * recv8, axis=0, keepdims=True) * S3 for m in range(3)
    ]
    two = [jnp.sum(q2[32 * m : 32 * m + 32] * recv8, axis=0, keepdims=True) for m in range(5)]
    dx = dd2 * x + one[0] + S15 * (two[0] * y + two[2] * z + two[3] * x) - S5 * two[4] * x
    dy = dd2 * y + one[1] + S15 * (two[0] * x + two[1] * z - two[3] * y) - S5 * two[4] * y
    dz = dd2 * z + one[2] + S15 * (two[1] * y + two[2] * x) + 2.0 * S5 * two[4] * z
    none = jnp.zeros_like(dx)
    drel_o[...] = jnp.concatenate([dx, dy, dz, none, none, none, none, none], axis=0)


def force_kernel(*refs):
    edges_all, folded, (dh2, seed1, e1, e2, wup_t, mix_t), v_all = refs[:3], refs[3], refs[4:10], refs[10:13]
    drel2, outs, rows = refs[13], refs[14:17], refs[17]
    rows[...] = jnp.zeros_like(rows)
    dh1 = product3(folded[...], wup_t[...])
    dh1 = jnp.concatenate([dh1[0:32], dh1[32:64] + dh2[...] + seed1[...], dh1[64:96]], axis=0)
    dp = product3(dh1, mix_t[0])
    for brick in range(3):
        start = 9 * brick
        edges, v = edges_all[brick], v_all[brick]
        hi, lo = split(dp[32 * brick : 32 * brick + 32])
        dp2 = jnp.concatenate([hi, lo], axis=0)
        sender = edges[0:1]
        recv = ones_at(edges[1:2], 32)
        slot = ones_at(jnp.bitwise_and(sender, 31), 32).astype(BF16)
        block = ones_at(jnp.right_shift(sender, 5), 32)
        spread, pulled = [], []
        for k in range(3):
            q = nn(dp2, v[128 * k : 128 * k + 128])
            q = q[0:32] + q[32:64]
            drel = jnp.sum(q * recv, axis=0, keepdims=True)
            if brick == 1:
                drel = drel + drel2[k : k + 1]
            force = drel * (-1.0 / cutoff_radius)
            hi, lo = split(force)
            hi, lo = hi.astype(F32), lo.astype(F32)
            spread += [block * hi, block * lo]
            pulled += [hi, lo]
        pushed = nt(jnp.concatenate(spread, axis=0).astype(BF16), slot)
        pulled = jnp.concatenate(pulled + [jnp.zeros_like(hi)] * 2, axis=0).astype(BF16)
        pulled = nt(pulled, recv.astype(BF16))
        middle = start + 13
        for k in range(3):
            lanes = slice(32 * k, 32 * k + 32)
            rows[start : start + 27, lanes] += (
                pushed[64 * k : 64 * k + 27] + pushed[64 * k + 32 : 64 * k + 59]
            )
            rows[middle : middle + 1, lanes] -= pulled[2 * k : 2 * k + 1] + pulled[2 * k + 1 : 2 * k + 2]
    rows[22:23, 96:128] = e1[...] + e2[0:1]
    for dx in range(5):
        for dy, out in enumerate(outs):
            out[3 * dx : 3 * dx + 3] = rows[9 * dx + 3 * dy : 9 * dx + 3 * dy + 3]


def spread_kernel(brick, a, b, c, out):
    out[...] = jnp.zeros_like(out)
    total = a[...] + b[...] + c[...]
    for k in range(15):
        out[pl.ds(around(brick, k), 1)] = total[k : k + 1]


def last_kernel(rows, energy_o, forces_o):
    atoms = energy_o.shape[-1]
    total = jnp.sum(rows[...], axis=0, keepdims=True)
    energy_o[0, 0] = total[:, 3 * atoms : 4 * atoms]
    for k in range(3):
        forces_o[k, 0, 0] = total[:, atoms * k : atoms * k + atoms]


def local(
    positions, species, atom_count, edge_count, sender, receiver, image_shift,
    embed, radial_in, radial_out, w_up, lam, w_mix, read_one, read_hidden, read_out,
):
    atoms = positions.shape[-1]
    count = sender.shape[-1]
    box = (SIDE * 4 * lattice_step, SIDE * 4 * lattice_step, SIDE * (atoms // 16) * lattice_step)

    brick = here()
    rows, edges = call(
        pack_kernel, [((SIDE * SIDE, 4 * atoms), F32), ((2, count), jnp.int32)],
        atom_count, edge_count, positions, species, sender, receiver, far=True,
        scratch=like(positions, species, sender, receiver),
    )
    edges = move(edges, bring_home())
    level = exchange(rows)

    weights = call(
        weights_kernel,
        [((128, 128), F32), ((128, 256), BF16), ((2, 64, 32), BF16), ((2, 384, 192), BF16),
         ((2, 64, 384), BF16), ((128, 256), BF16), ((2, 384, 128), BF16), ((2, 384, 128), BF16), ((384, 128), BF16),
         ((384, 16), BF16), ((2, 2, 128), F32), ((1, 128), F32), ((16, 128), F32), ((1, 16), F32)],
        embed, radial_in, radial_out, w_up, w_mix, lam, read_one[None], read_hidden.T, read_out[None],
        far=True, scratch=like(embed, radial_in, radial_out, w_up, w_mix),
    )
    level, weights, edges = lax.optimization_barrier((level, weights, edges))
    emb, t0, win, wout, woutb, wup, mix, mix_t, wup_t, hidden_w, lam, read_one, read_hidden, read_out = weights
    below, level, above = widen(level, 1)
    edges, above = lax.optimization_barrier((edges, above))
    before, edges, after = widen(edges, 0)
    edges = (before, edges, after)

    results = [((8, count), F32), ((288, count), BF16), ((256, 128), BF16), ((128, count), BF16),
               ((384, count), BF16)]
    e1, seed1, seed2, h1, parts, table, *own = call(
        functools.partial(own_kernel, box),
        [((1, 32), F32), ((32, 128), F32), ((32, 16), F32), ((32, 128), BF16), ((4, 56, 96), F32),
         ((56, 128), F32)] + results,
        brick, below, level, above, edges[1], emb, t0, win, wout, lam, mix, read_one, read_out,
        index=True,
    )
    h1, *sides = call(
        functools.partial(sides_kernel, box), [((96, 128), BF16)] + results * 2,
        edges[0], edges[2], parts, table, h1, emb, t0, win, wout, lam, mix,
    )
    per_brick = (sides[:5], own, sides[5:])
    geo, pool = per_brick[1][:2]

    def direction(brick, found=None):
        found = per_brick[brick] if found is None else found
        return call(
            direction_kernel, [((384, count), BF16)], edges[brick], *found, win, wout,
            flops=1_000_000_000,
        )[0]

    hidden = call(
        radial_kernel,
        [((864, count), BF16), ((384, count), F32), ((64, count), F32)],
        edges[1], geo, win, wout, flops=1_000_000_000,
    )
    plane = jnp.concatenate(widen(h1, 1), axis=0)
    plane, (hotref, rad, slope) = lax.optimization_barrier((plane, hidden))
    left, own, right = widen(plane, 2)
    left, right, v_own = lax.optimization_barrier((left, right, direction(1)))

    dleft, down, dright, dh2, e2, drad, base2, da = call(
        second_kernel,
        [((288, 128), BF16), ((288, 128), F32), ((288, 128), BF16), ((32, 128), F32), ((8, 32), F32),
         ((384, count), BF16), ((384, count), BF16), ((288, 128), BF16)],
        left, own, right, hotref, rad, pool, wup, lam, mix, mix_t, hidden_w, read_hidden, seed2,
    )
    dh2, before = lax.optimization_barrier((dh2, per_brick[0]))
    v_before = direction(0, before)

    plane = down + move(dleft, shift(2, 1)).astype(F32) + move(dright, shift(2, -1)).astype(F32)
    plane, v_before, after = lax.optimization_barrier((plane, v_before, per_brick[2]))
    v_after = direction(2, after)
    folded = (
        plane[96:192]
        + move(plane[0:96].astype(BF16), shift(1, 1)).astype(F32)
        + move(plane[192:288].astype(BF16), shift(1, -1)).astype(F32)
    )

    (drel2,) = call(
        slope_kernel, [((8, count), F32)], edges[1], geo, slope, drad, base2, da, woutb,
        flops=1_000_000_000,
    )

    below, level, above = call(
        force_kernel, [((15, 128), F32)] * 3,
        *edges, folded, dh2, seed1, e1, e2, wup_t, mix_t, v_before, v_own, v_after, drel2,
        scratch=[pltpu.VMEM((48, 128), F32)],
    )

    (rows,) = call(
        spread_kernel, [((SIDE * SIDE, 4 * atoms), F32)],
        brick, level, move(below, shift(1, 1)), move(above, shift(1, -1)), index=True,
    )
    return call(
        last_kernel, [((1, 1, 1, atoms), F32), ((3, 1, 1, 1, atoms), F32)], exchange(rows)
    )


def solution(mesh):
    cell = P("gx", "gy", "gz")
    in_specs = (
        P(None, "gx", "gy", "gz", None),
        P("gx", "gy", "gz", None),
        cell,
        cell,
        P("gx", "gy", "gz", None),
        P("gx", "gy", "gz", None),
        P(None, "gx", "gy", "gz", None),
    ) + (P(),) * 9
    out_specs = (P("gx", "gy", "gz", None), P(None, "gx", "gy", "gz", None))
    return jax.shard_map(local, mesh=mesh, in_specs=in_specs, out_specs=out_specs, check_vma=False)
```

```python
import functools

import jax
import jax.numpy as jnp
import numpy as np
from jax import lax
from jax.experimental import pallas as pl
from jax.experimental.pallas import tpu as pltpu
from jax.sharding import PartitionSpec as P

cutoff_radius = 5.0
lattice_step = 2.25
AXES = ("gx", "gy", "gz")
SIDE = 8
F32 = jnp.float32
BF16 = jnp.bfloat16
S3 = 3.0**0.5
S5 = 5.0**0.5
S15 = 15.0**0.5
HIGH = lax.Precision.HIGHEST


def place(a, b, d):
    return (a * SIDE + b) * SIDE + d


def home(a, b, d):
    return place((a % 4) * 2 + d % 2, b, (d // 2) * 2 + a // 4)


def bricks():
    return [(a, b, d) for a in range(SIDE) for b in range(SIDE) for d in range(SIDE)]


def move(x, pairs):
    return lax.ppermute(x, AXES, pairs)


def bring_home():
    return [(place(a, b, d), home(a, b, d)) for a, b, d in bricks()]


def around():
    gx, gz = lax.axis_index("gx"), lax.axis_index("gz")
    a, d = (gz % 2) * 4 + gx // 2, (gz // 2) * 2 + gx % 2
    k = lax.broadcasted_iota(jnp.int32, (16, SIDE * SIDE), 0)
    at = lax.broadcasted_iota(jnp.int32, (16, SIDE * SIDE), 1)
    i = k // 3
    place_k = ((a + i + SIDE - 2) % SIDE) * SIDE + (d + k - 3 * i + SIDE - 1) % SIDE
    return jnp.where((place_k == at) & (k < 15), 1.0, 0.0).astype(F32)


def exchange(x):
    rows = x.reshape(x.shape[0], 1, x.shape[1])
    return lax.all_to_all(rows, ("gx", "gz"), 0, 0, tiled=True).reshape(x.shape)


def shift(axis, step):
    pairs = []
    for cell in bricks():
        other = list(cell)
        other[axis] = (other[axis] + step) % SIDE
        pairs.append((home(*other), home(*cell)))
    return pairs


def widen(x, axis):
    return [move(x, shift(axis, -1)), x, move(x, shift(axis, 1))]


def nn(a, b, **kw):
    return lax.dot_general(a, b, (((1,), (0,)), ((), ())), preferred_element_type=F32, **kw)


def nt(a, b, **kw):
    return lax.dot_general(a, b, (((1,), (1,)), ((), ())), preferred_element_type=F32, **kw)


def tn(a, b, **kw):
    return lax.dot_general(a, b, (((0,), (0,)), ((), ())), preferred_element_type=F32, **kw)


def split(x):
    hi = x.astype(BF16)
    return hi, (x - hi.astype(F32)).astype(BF16)


def stack3(x):
    hi, lo = split(x)
    return jnp.concatenate([hi, lo, hi], axis=0)


def product3(x, stack):
    hi, lo = split(x)
    return nn(jnp.concatenate([hi, lo, hi], axis=1), stack)


def rows3(w):
    hi, lo = split(w)
    return jnp.concatenate([hi, hi, lo], axis=0)


def hot(index, rows):
    edges = index.shape[1]
    return lax.broadcasted_iota(jnp.int32, (rows, edges), 0) == index


def ones_at(index, rows):
    return jnp.where(hot(index, rows), 1.0, 0.0).astype(F32)


def small_stack(x):
    hi, lo = split(x)
    hi, lo = hi.astype(F32), lo.astype(F32)
    return jnp.concatenate([hi, lo, hi, jnp.zeros_like(x)], axis=0).astype(BF16)


def hidden_units(d2, env, denv, win):
    edges = d2.shape[1]
    centre = lax.broadcasted_iota(jnp.int32, (8, edges), 0).astype(F32) * (1.0 / 7.0)
    gap = d2 - centre
    basis = jnp.exp(-64.0 * gap * gap)
    slope = basis * (-128.0 * gap)
    pre = nn(win, small_stack(basis))
    dpre = nn(win, small_stack(slope))
    sig = 1.0 / (1.0 + jnp.exp(-pre))
    act = pre * sig
    dact = sig * (1.0 + pre * (1.0 - sig)) * dpre
    return act * env, dact * env + act * denv


def call(kernel, outs, *args, flops=1_000_000, limit=16, scratch=(), far=False):
    params = {}
    if far:
        spaces = [pltpu.SMEM if a.size == 1 else pltpu.HBM for a in args]
        args = [
            a if s is pltpu.SMEM else pltpu.with_memory_space_constraint(a, s)
            for a, s in zip(args, spaces)
        ]
        params["in_specs"] = [pl.BlockSpec(memory_space=s) for s in spaces]
        scratch = list(scratch) + [pltpu.SemaphoreType.DMA((len(args),))]
    return pl.pallas_call(
        kernel,
        out_shape=tuple(jax.ShapeDtypeStruct(s, d) for s, d in outs),
        scratch_shapes=scratch,
        compiler_params=pltpu.CompilerParams(vmem_limit_bytes=limit * 1024 * 1024),
        cost_estimate=pl.CostEstimate(flops=flops, bytes_accessed=1_000_000, transcendentals=0),
        **params,
    )(*args)


def fetch(sources, targets, sems):
    copies = [
        pltpu.make_async_copy(s, t, sems.at[i]) for i, (s, t) in enumerate(zip(sources, targets))
    ]
    for copy in copies:
        copy.start()
    for copy in copies:
        copy.wait()


def like(*args):
    return [pltpu.VMEM(a.shape, a.dtype) for a in args]


def pack_kernel(*refs):
    (atom_count, edge_count), far, (rows_o, edges_o) = refs[:2], refs[2:6], refs[6:8]
    near, sems = refs[8:12], refs[12]
    fetch(far, near, sems)
    positions, species, sender, receiver = near
    atoms, count = species.shape[-1], sender.shape[-1]
    owned = lax.broadcasted_iota(jnp.int32, (1, atoms), 1) < atom_count[0, 0, 0]
    kinds = jnp.where(owned, species[0, 0], -1).astype(F32)
    for c, part in enumerate([positions[k, 0, 0] for k in range(3)] + [kinds]):
        rows_o[0:1, atoms * c : atoms * c + atoms] = part
    rows_o[...] = jnp.broadcast_to(rows_o[0:1], rows_o.shape)
    live = lax.broadcasted_iota(jnp.int32, (1, count), 1) < edge_count[0, 0, 0]
    s, r = sender[0, 0], receiver[0, 0]
    edges_o[0:1] = jnp.where(live, s, 1023)
    edges_o[1:2] = jnp.where(live, r, 99)


def weights_kernel(*refs):
    far, outs, near, sems = refs[:9], refs[9:23], refs[23:28], refs[28]
    (emb_o, t0_o, win_o, wout_o, woutb_o, wup_o, mix_o, mixt_o, wupt_o, hw_o), kept = outs[:10], outs[10:]
    fetch(far, list(near) + list(kept), sems)
    embed, rin, rout, wup, wmix = near
    wupt_o[...] = rows3(wup[1].T)
    for t in range(2):
        mix_o[t] = rows3(wmix[t])
        mixt_o[t] = rows3(wmix[t].T)
    hw_o[...] = rows3(kept[2][...].T)
    emb_o[...] = jnp.zeros_like(emb_o)
    emb_o[0 : embed.shape[0]] = embed[...].astype(BF16).astype(F32)
    table = nn(emb_o[...], wup[0], precision=HIGH)
    hi, lo = split(table.T)
    t0_o[...] = jnp.concatenate([hi, lo], axis=1)
    for t in range(2):
        hi, lo = split(rin[t])
        hi, lo = hi.astype(F32), lo.astype(F32)
        both = jnp.concatenate([hi, hi, lo, jnp.zeros_like(hi)], axis=0)
        win_o[t] = both.T.astype(BF16)
        hi, lo = split(rout[t])
        woutb_o[t] = hi
        hi, lo = hi.astype(F32), lo.astype(F32)
        both = jnp.concatenate([hi, hi, lo], axis=0)
        wout_o[t] = both.T.astype(BF16)
    hi, lo = split(wup[1].T)
    wup_o[...] = jnp.concatenate([hi, lo], axis=1)


def own_kernel(box, *refs):
    (chosen, below, level, above, edges), weights = refs[:5], refs[5:11]
    (mask_o, full_o, h1_o, parts, table), results = refs[11:16], refs[16:21]
    table[...] = jnp.zeros_like(table)
    for dy, plane in enumerate((below, level, above)):
        near = nn(chosen[...], plane[...], precision=HIGH)
        for i in range(5):
            table[9 * i + 3 * dy : 9 * i + 3 * dy + 3] = near[3 * i : 3 * i + 3]
    rows = table[...]
    hi = rows.astype(BF16).astype(F32)
    rest = rows - hi
    mid = rest.astype(BF16).astype(F32)
    low = rest - mid
    for c in range(4):
        parts[c] = jnp.concatenate([p[:, 32 * c : 32 * c + 32] for p in (hi, mid, low)], axis=1)
    h1, mask = first_layer(box, 9, edges, *weights, *results, table, parts)
    h1_o[...] = h1.astype(BF16)
    full_o[...] = h1
    mask_o[...] = mask


def sides_kernel(box, before, after, parts, table, h1, *refs):
    weights, h1_o, results = refs[:6], refs[6], refs[7:]
    h1_o[32:64] = h1[...]
    for brick, edges in ((0, before), (2, after)):
        found = results[:5] if brick == 0 else results[5:]
        value, _ = first_layer(box, 9 * brick, edges, *weights, *found, table, parts)
        h1_o[32 * brick : 32 * brick + 32] = value.astype(BF16)


def first_layer(
    box, start, edges, emb, t0, win, wout, lam, mix, geo_o, pool_o, at_o, lift_o, base_o, table, parts
):
    lhs = jnp.concatenate([parts[c, start : start + 32] for c in range(4)], axis=0).astype(BF16)
    middle = start + 13
    mine = [parts[c, middle : middle + 1] for c in range(4)] + [jnp.zeros((4, 96), F32)]
    mine = jnp.concatenate(mine, axis=0)
    sender = edges[0:1]
    receiver = edges[1:2]
    slot = ones_at(jnp.bitwise_and(sender, 31), 32).astype(BF16)
    block = ones_at(jnp.right_shift(sender, 5), 32)
    recv = ones_at(receiver, 32)
    recv_b = recv.astype(BF16)
    got = nn(lhs, jnp.concatenate([slot] * 3, axis=0))
    at_recv = nn(mine.astype(BF16), jnp.concatenate([recv_b] * 3, axis=0))
    sent = [jnp.sum(got[32 * c : 32 * c + 32] * block, axis=0, keepdims=True) for c in range(4)]
    rel = []
    for c in range(3):
        d = sent[c] - at_recv[c : c + 1]
        d = d - jnp.round(d * (1.0 / box[c])) * box[c]
        rel.append(d * (1.0 / cutoff_radius))
    x, y, z = rel
    d2 = x * x + y * y + z * z
    reach = jnp.maximum(1.0 - d2, 0.0)
    env = reach * reach
    denv = -2.0 * reach
    geo_o[...] = jnp.concatenate([x, y, z, d2, env, denv, d2, d2], axis=0)
    harmonics = [
        jnp.ones_like(x),
        S3 * x,
        S3 * y,
        S3 * z,
        S15 * x * y,
        S15 * y * z,
        S15 * x * z,
        0.5 * S15 * (x * x - y * y),
        0.5 * S5 * (2.0 * z * z - x * x - y * y),
    ]
    for m, value in enumerate(harmonics):
        pool_o[32 * m : 32 * m + 32] = (recv * (value * 0.125)).astype(BF16)
    hidden, _ = hidden_units(d2, env, denv, win[0])
    radial = nn(wout[0], stack3(hidden))
    kind = ones_at(sent[3].astype(jnp.int32), 128).astype(BF16)
    lift = nn(t0[...], jnp.concatenate([kind, kind], axis=0))
    lift_o[...] = lift.astype(BF16)
    sums = []
    for order, (a, b) in enumerate(((0, 32), (32, 128), (128, 288))):
        base = (radial[128 * order : 128 * order + 128] * lift).astype(BF16)
        base_o[128 * order : 128 * order + 128] = base
        sums.append(nt(pool_o[a:b], base))
    product = sums[0]
    for order in (1, 2):
        total = sums[order]
        weight = lam[0, order - 1 : order]
        square = sum(
            total[32 * m : 32 * m + 32] * total[32 * m : 32 * m + 32]
            for m in range(2 * order + 1)
        )
        product = product + weight * square
        first = 0 if order == 1 else 96
        at_o[first : first + 32 * (2 * order + 1)] = (2.0 * weight * total).astype(BF16)
    kinds = table[middle : middle + 1, 96:128]
    mask = jnp.where(kinds >= 0.0, 1.0, 0.0)
    own_kind = jnp.where(
        lax.broadcasted_iota(jnp.int32, (128, 32), 0) == kinds.astype(jnp.int32), 1.0, 0.0
    ).astype(BF16)
    h0 = tn(own_kind, emb[...].astype(BF16))
    return h0 + product3(product, mix[0]), mask


def radial_kernel(
    edges, geo, win, wout, mask, h1, read_one, read_out, hot_o, rad_o, slope_o, e1_o, seed1_o, seed2_o
):
    s = edges[0:1]
    block, slot = jnp.right_shift(s, 5), jnp.bitwise_and(s, 31)
    one = lambda flag: jnp.where(flag, 1, 0)
    bx = one(block >= 9) + one(block >= 18)
    block = block - 9 * bx
    by = one(block >= 3) + one(block >= 6)
    bz = block - 3 * by
    s = (bz * 9 + by * 3 + bx) * 32 + slot
    sender = s
    for r in range(0, 864, 96):
        row = lax.broadcasted_iota(jnp.int32, (96, sender.shape[1]), 0) + r
        hot_o[r : r + 96] = jnp.where(row == sender, 1.0, 0.0).astype(BF16)
    hidden, slope = hidden_units(geo[3:4], geo[4:5], geo[5:6], win[1])
    rad_o[...] = nn(wout[1], stack3(hidden))
    slope_o[...] = slope
    e1_o[...] = nt(read_one[...], h1[...], precision=HIGH) * mask[...]
    mask8 = jnp.concatenate([mask[...], jnp.zeros((7, 32), F32)], axis=0)
    zero = lax.broadcasted_iota(jnp.int32, (8, 128), 0) == 0
    seed1_o[...] = tn(mask8, jnp.where(zero, read_one[...], 0.0), precision=HIGH)
    zero = lax.broadcasted_iota(jnp.int32, (8, 16), 0) == 0
    seed2_o[...] = tn(mask8, jnp.where(zero, read_out[...], 0.0), precision=HIGH)


def direction_kernel(edges, geo, pool, at, lift, base, win, wout, v_o):
    x, y, z = geo[0:1], geo[1:2], geo[2:3]
    recv = ones_at(edges[1:2], 32)
    _, slope = hidden_units(geo[3:4], geo[4:5], geo[5:6], win[0])
    drad = nn(wout[0], stack3(slope))
    g1 = tn(at[0:96], pool[32:128])
    g2 = tn(at[96:256], pool[128:288])
    common = drad[0:128] * 0.125 + drad[128:256] * g1 + drad[256:384] * g2
    common = lift[...].astype(F32) * common
    b1 = base[128:256].astype(F32)
    b2 = base[256:384].astype(F32)
    recv8 = recv * 0.125
    turns = (
        ((0, S15 * y), (2, S15 * z), (3, S15 * x), (4, -S5 * x)),
        ((0, S15 * x), (1, S15 * z), (3, -S15 * y), (4, -S5 * y)),
        ((1, S15 * y), (2, S15 * x), (4, 2.0 * S5 * z)),
    )
    for k, coordinate in enumerate((x, y, z)):
        h1 = tn(at[32 * k : 32 * k + 32], (recv8 * S3).astype(BF16))
        left = jnp.concatenate([at[96 + 32 * m : 128 + 32 * m] for m, _ in turns[k]], axis=0)
        right = jnp.concatenate([(recv8 * f).astype(BF16) for _, f in turns[k]], axis=0)
        h2 = tn(left, right)
        v = common * (2.0 * coordinate) + b1 * h1 + b2 * h2
        v_o[128 * k : 128 * k + 128] = v.astype(BF16)


def second_kernel(
    left, own, right, hotref, rad, pool, wup, lam, mix, mix_t, hidden_w, read_hidden, seed2,
    dleft_o, down_o, dright_o, dh2_o, e2_o, drad_o, base_o, da_o,
):
    feats = jnp.concatenate([left[...], own[...], right[...]], axis=0)
    got = tn(feats, hotref[...]).astype(BF16)
    lift = nn(wup[...], jnp.concatenate([got, got], axis=0))
    sums = []
    spans = ((0, 32), (32, 128), (128, 288))
    for order, (a, b) in enumerate(spans):
        base = (rad[128 * order : 128 * order + 128] * lift).astype(BF16)
        base_o[128 * order : 128 * order + 128] = base
        sums.append(nt(pool[a:b], base))
    product = sums[0]
    for order in (1, 2):
        total = sums[order]
        square = sum(
            total[32 * m : 32 * m + 32] * total[32 * m : 32 * m + 32]
            for m in range(2 * order + 1)
        )
        product = product + lam[1, order - 1 : order] * square
    h2 = own[128:160].astype(F32) + product3(product, mix[1])
    pre = product3(h2, hidden_w[...])
    sig = 1.0 / (1.0 + jnp.exp(-pre))
    inner = pre * sig
    seed = seed2[...]
    e2_o[...] = nt(jnp.ones((8, 16), F32), inner * seed, precision=HIGH)
    dpre = seed * sig * (1.0 + pre * (1.0 - sig))
    dh2 = nn(dpre, read_hidden[...], precision=HIGH)
    dh2_o[...] = dh2
    dp = product3(dh2, mix_t[1])
    da_o[0:32] = dp.astype(BF16)
    for order in (1, 2):
        weight = 2.0 * lam[1, order - 1 : order] * dp
        a = spans[order][0]
        for m in range(2 * order + 1):
            piece = weight * sums[order][32 * m : 32 * m + 32]
            da_o[a + 32 * m : a + 32 * m + 32] = piece.astype(BF16)
    dlift = None
    for order, (a, b) in enumerate(spans):
        g = tn(da_o[a:b], pool[a:b])
        drad_o[128 * order : 128 * order + 128] = (lift * g).astype(BF16)
        term = rad[128 * order : 128 * order + 128] * g
        dlift = term if dlift is None else dlift + term
    hi, lo = split(dlift)
    back = nt(hotref[...], jnp.concatenate([hi, lo], axis=0))
    back = back[:, 0:128] + back[:, 128:256]
    dleft_o[...] = back[0:288].astype(BF16)
    down_o[...] = back[288:576]
    dright_o[...] = back[576:864].astype(BF16)


def slope_kernel(edges, geo, slope, drad, base, da, woutb, drel_o):
    x, y, z = geo[0:1], geo[1:2], geo[2:3]
    recv8 = ones_at(edges[1:2], 32) * 0.125
    dhidden = nn(woutb[1], drad[...])
    dd2 = 2.0 * jnp.sum(dhidden * slope[...], axis=0, keepdims=True)
    q1 = nn(da[32:128], base[128:256])
    q2 = nn(da[128:288], base[256:384])
    one = [
        jnp.sum(q1[32 * m : 32 * m + 32] * recv8, axis=0, keepdims=True) * S3 for m in range(3)
    ]
    two = [jnp.sum(q2[32 * m : 32 * m + 32] * recv8, axis=0, keepdims=True) for m in range(5)]
    dx = dd2 * x + one[0] + S15 * (two[0] * y + two[2] * z + two[3] * x) - S5 * two[4] * x
    dy = dd2 * y + one[1] + S15 * (two[0] * x + two[1] * z - two[3] * y) - S5 * two[4] * y
    dz = dd2 * z + one[2] + S15 * (two[1] * y + two[2] * x) + 2.0 * S5 * two[4] * z
    none = jnp.zeros_like(dx)
    drel_o[...] = jnp.concatenate([dx, dy, dz, none, none, none, none, none], axis=0)


def force_kernel(*refs):
    edges_all, folded, (dh2, seed1, e1, e2, wup_t, mix_t), v_all = refs[:3], refs[3], refs[4:10], refs[10:13]
    drel2, outs, rows = refs[13], refs[14:17], refs[17]
    rows[...] = jnp.zeros_like(rows)
    dh1 = product3(folded[...], wup_t[...])
    dh1 = jnp.concatenate([dh1[0:32], dh1[32:64] + dh2[...] + seed1[...], dh1[64:96]], axis=0)
    dp = product3(dh1, mix_t[0])
    for brick in range(3):
        start = 9 * brick
        edges, v = edges_all[brick], v_all[brick]
        hi, lo = split(dp[32 * brick : 32 * brick + 32])
        dp2 = jnp.concatenate([hi, lo], axis=0)
        sender = edges[0:1]
        recv = ones_at(edges[1:2], 32)
        slot = ones_at(jnp.bitwise_and(sender, 31), 32).astype(BF16)
        block = ones_at(jnp.right_shift(sender, 5), 32)
        spread, pulled = [], []
        for k in range(3):
            q = nn(dp2, v[128 * k : 128 * k + 128])
            q = q[0:32] + q[32:64]
            drel = jnp.sum(q * recv, axis=0, keepdims=True)
            if brick == 1:
                drel = drel + drel2[k : k + 1]
            force = drel * (-1.0 / cutoff_radius)
            hi, lo = split(force)
            hi, lo = hi.astype(F32), lo.astype(F32)
            spread += [block * hi, block * lo]
            pulled += [hi, lo]
        pushed = nt(jnp.concatenate(spread, axis=0).astype(BF16), slot)
        pulled = jnp.concatenate(pulled + [jnp.zeros_like(hi)] * 2, axis=0).astype(BF16)
        pulled = nt(pulled, recv.astype(BF16))
        middle = start + 13
        for k in range(3):
            lanes = slice(32 * k, 32 * k + 32)
            rows[start : start + 27, lanes] += (
                pushed[64 * k : 64 * k + 27] + pushed[64 * k + 32 : 64 * k + 59]
            )
            rows[middle : middle + 1, lanes] -= pulled[2 * k : 2 * k + 1] + pulled[2 * k + 1 : 2 * k + 2]
    rows[22:23, 96:128] = e1[...] + e2[0:1]
    for dx in range(5):
        for dy, out in enumerate(outs):
            out[3 * dx : 3 * dx + 3] = rows[9 * dx + 3 * dy : 9 * dx + 3 * dy + 3]
    for out in outs:
        out[15:16] = jnp.zeros((1, 128), F32)


def spread_kernel(chosen, a, b, c, out):
    out[...] = tn(chosen[...], a[...] + b[...] + c[...], precision=HIGH)


def last_kernel(rows, energy_o, forces_o):
    atoms = energy_o.shape[-1]
    total = jnp.sum(rows[...], axis=0, keepdims=True)
    energy_o[0, 0] = total[:, 3 * atoms : 4 * atoms]
    for k in range(3):
        forces_o[k, 0, 0] = total[:, atoms * k : atoms * k + atoms]


def local(
    positions, species, atom_count, edge_count, sender, receiver, image_shift,
    embed, radial_in, radial_out, w_up, lam, w_mix, read_one, read_hidden, read_out,
):
    atoms = positions.shape[-1]
    count = sender.shape[-1]
    box = (SIDE * 4 * lattice_step, SIDE * 4 * lattice_step, SIDE * (atoms // 16) * lattice_step)

    chosen = around()
    rows, edges = call(
        pack_kernel, [((SIDE * SIDE, 4 * atoms), F32), ((2, count), jnp.int32)],
        atom_count, edge_count, positions, species, sender, receiver, far=True,
        scratch=like(positions, species, sender, receiver),
    )
    edges = move(edges, bring_home())
    level = exchange(rows)

    weights = call(
        weights_kernel,
        [((128, 128), F32), ((128, 256), BF16), ((2, 64, 32), BF16), ((2, 384, 192), BF16),
         ((2, 64, 384), BF16), ((128, 256), BF16), ((2, 384, 128), BF16), ((2, 384, 128), BF16), ((384, 128), BF16),
         ((384, 16), BF16), ((2, 2, 128), F32), ((1, 128), F32), ((16, 128), F32), ((1, 16), F32)],
        embed, radial_in, radial_out, w_up, w_mix, lam, read_one[None], read_hidden.T, read_out[None],
        far=True, scratch=like(embed, radial_in, radial_out, w_up, w_mix),
    )
    level, weights, edges = lax.optimization_barrier((level, weights, edges))
    emb, t0, win, wout, woutb, wup, mix, mix_t, wup_t, hidden_w, lam, read_one, read_hidden, read_out = weights
    below, level, above = widen(level, 1)
    edges, above = lax.optimization_barrier((edges, above))
    before, edges, after = widen(edges, 0)
    edges = (before, edges, after)

    results = [((8, count), F32), ((288, count), BF16), ((256, 128), BF16), ((128, count), BF16),
               ((384, count), BF16)]
    mask, h1_full, h1, parts, table, *own = call(
        functools.partial(own_kernel, box),
        [((1, 32), F32), ((32, 128), F32), ((32, 128), BF16), ((4, 56, 96), F32), ((56, 128), F32)]
        + results,
        chosen, below, level, above, edges[1], emb, t0, win, wout, lam, mix,
    )
    h1, *sides = call(
        functools.partial(sides_kernel, box), [((96, 128), BF16)] + results * 2,
        edges[0], edges[2], parts, table, h1, emb, t0, win, wout, lam, mix,
    )
    per_brick = (sides[:5], own, sides[5:])
    geo, pool = per_brick[1][:2]

    def direction(brick, found=None):
        found = per_brick[brick] if found is None else found
        return call(
            direction_kernel, [((384, count), BF16)], edges[brick], *found, win, wout,
            flops=1_000_000_000,
        )[0]

    hidden = call(
        radial_kernel,
        [((864, count), BF16), ((384, count), F32), ((64, count), F32), ((1, 32), F32), ((32, 128), F32),
         ((32, 16), F32)],
        edges[1], geo, win, wout, mask, h1_full, read_one, read_out, flops=1_000_000_000,
    )
    plane = jnp.concatenate(widen(h1, 1), axis=0)
    plane, (hotref, rad, slope, e1, seed1, seed2) = lax.optimization_barrier((plane, hidden))
    left, own, right = widen(plane, 2)
    left, right, v_own = lax.optimization_barrier((left, right, direction(1)))

    dleft, down, dright, dh2, e2, drad, base2, da = call(
        second_kernel,
        [((288, 128), BF16), ((288, 128), F32), ((288, 128), BF16), ((32, 128), F32), ((8, 32), F32),
         ((384, count), BF16), ((384, count), BF16), ((288, 128), BF16)],
        left, own, right, hotref, rad, pool, wup, lam, mix, mix_t, hidden_w, read_hidden, seed2,
    )
    dh2, before = lax.optimization_barrier((dh2, per_brick[0]))
    v_before = direction(0, before)

    plane = down + move(dleft, shift(2, 1)).astype(F32) + move(dright, shift(2, -1)).astype(F32)
    plane, v_before, after = lax.optimization_barrier((plane, v_before, per_brick[2]))
    v_after = direction(2, after)
    folded = (
        plane[96:192]
        + move(plane[0:96].astype(BF16), shift(1, 1)).astype(F32)
        + move(plane[192:288].astype(BF16), shift(1, -1)).astype(F32)
    )

    (drel2,) = call(
        slope_kernel, [((8, count), F32)], edges[1], geo, slope, drad, base2, da, woutb,
        flops=1_000_000_000,
    )

    below, level, above = call(
        force_kernel, [((16, 128), F32)] * 3,
        *edges, folded, dh2, seed1, e1, e2, wup_t, mix_t, v_before, v_own, v_after, drel2,
        scratch=[pltpu.VMEM((48, 128), F32)],
    )

    (rows,) = call(
        spread_kernel, [((SIDE * SIDE, 4 * atoms), F32)],
        chosen, level, move(below, shift(1, 1)), move(above, shift(1, -1)),
    )
    return call(
        last_kernel, [((1, 1, 1, atoms), F32), ((3, 1, 1, 1, atoms), F32)], exchange(rows)
    )


def solution(mesh):
    cell = P("gx", "gy", "gz")
    in_specs = (
        P(None, "gx", "gy", "gz", None),
        P("gx", "gy", "gz", None),
        cell,
        cell,
        P("gx", "gy", "gz", None),
        P("gx", "gy", "gz", None),
        P(None, "gx", "gy", "gz", None),
    ) + (P(),) * 9
    out_specs = (P("gx", "gy", "gz", None), P(None, "gx", "gy", "gz", None))
    return jax.shard_map(local, mesh=mesh, in_specs=in_specs, out_specs=out_specs, check_vma=False)
```

```python
import functools

import jax
import jax.numpy as jnp
import numpy as np
from jax import lax
from jax.experimental import pallas as pl
from jax.experimental.pallas import tpu as pltpu
from jax.sharding import PartitionSpec as P

cutoff_radius = 5.0
lattice_step = 2.25
AXES = ("gx", "gy", "gz")
SIDE = 8
F32 = jnp.float32
BF16 = jnp.bfloat16
S3 = 3.0**0.5
S5 = 5.0**0.5
S15 = 15.0**0.5
HIGH = lax.Precision.HIGHEST


def place(a, b, d):
    return (a * SIDE + b) * SIDE + d


def home(a, b, d):
    return place((a % 4) * 2 + d % 2, b, (d // 2) * 2 + a // 4)


def bricks():
    return [(a, b, d) for a in range(SIDE) for b in range(SIDE) for d in range(SIDE)]


def move(x, pairs):
    return lax.ppermute(x, AXES, pairs)


def bring_home():
    return [(place(a, b, d), home(a, b, d)) for a, b, d in bricks()]


def around():
    gx, gz = lax.axis_index("gx"), lax.axis_index("gz")
    a, d = (gz % 2) * 4 + gx // 2, (gz // 2) * 2 + gx % 2
    k = lax.broadcasted_iota(jnp.int32, (16, SIDE * SIDE), 0)
    at = lax.broadcasted_iota(jnp.int32, (16, SIDE * SIDE), 1)
    i = k // 3
    place_k = ((a + i + SIDE - 2) % SIDE) * SIDE + (d + k - 3 * i + SIDE - 1) % SIDE
    return jnp.where((place_k == at) & (k < 15), 1.0, 0.0).astype(F32)


def exchange(x):
    rows = x.reshape(x.shape[0], 1, x.shape[1])
    return lax.all_to_all(rows, ("gx", "gz"), 0, 0, tiled=True).reshape(x.shape)


def shift(axis, step):
    pairs = []
    for cell in bricks():
        other = list(cell)
        other[axis] = (other[axis] + step) % SIDE
        pairs.append((home(*other), home(*cell)))
    return pairs


def widen(x, axis):
    return [move(x, shift(axis, -1)), x, move(x, shift(axis, 1))]


def nn(a, b, **kw):
    return lax.dot_general(a, b, (((1,), (0,)), ((), ())), preferred_element_type=F32, **kw)


def nt(a, b, **kw):
    return lax.dot_general(a, b, (((1,), (1,)), ((), ())), preferred_element_type=F32, **kw)


def tn(a, b, **kw):
    return lax.dot_general(a, b, (((0,), (0,)), ((), ())), preferred_element_type=F32, **kw)


def split(x):
    hi = x.astype(BF16)
    return hi, (x - hi.astype(F32)).astype(BF16)


def stack3(x):
    hi, lo = split(x)
    return jnp.concatenate([hi, lo, hi], axis=0)


def product3(x, stack):
    hi, lo = split(x)
    return nn(jnp.concatenate([hi, lo, hi], axis=1), stack)


def rows3(w):
    hi, lo = split(w)
    return jnp.concatenate([hi, hi, lo], axis=0)


def hot(index, rows):
    edges = index.shape[1]
    return lax.broadcasted_iota(jnp.int32, (rows, edges), 0) == index


def ones_at(index, rows):
    return jnp.where(hot(index, rows), 1.0, 0.0).astype(F32)


def small_stack(x):
    hi, lo = split(x)
    hi, lo = hi.astype(F32), lo.astype(F32)
    return jnp.concatenate([hi, lo, hi, jnp.zeros_like(x)], axis=0).astype(BF16)


def hidden_units(d2, env, denv, win):
    edges = d2.shape[1]
    centre = lax.broadcasted_iota(jnp.int32, (8, edges), 0).astype(F32) * (1.0 / 7.0)
    gap = d2 - centre
    basis = jnp.exp(-64.0 * gap * gap)
    slope = basis * (-128.0 * gap)
    pre = nn(win, small_stack(basis))
    dpre = nn(win, small_stack(slope))
    sig = 1.0 / (1.0 + jnp.exp(-pre))
    act = pre * sig
    dact = sig * (1.0 + pre * (1.0 - sig)) * dpre
    return act * env, dact * env + act * denv


def call(kernel, outs, *args, flops=1_000_000, limit=16, scratch=(), far=False):
    params = {}
    if far:
        spaces = [pltpu.SMEM if a.size == 1 else pltpu.HBM for a in args]
        args = [
            a if s is pltpu.SMEM else pltpu.with_memory_space_constraint(a, s)
            for a, s in zip(args, spaces)
        ]
        params["in_specs"] = [pl.BlockSpec(memory_space=s) for s in spaces]
        scratch = list(scratch) + [pltpu.SemaphoreType.DMA((len(args),))]
    return pl.pallas_call(
        kernel,
        out_shape=tuple(jax.ShapeDtypeStruct(s, d) for s, d in outs),
        scratch_shapes=scratch,
        compiler_params=pltpu.CompilerParams(vmem_limit_bytes=limit * 1024 * 1024),
        cost_estimate=pl.CostEstimate(flops=flops, bytes_accessed=1_000_000, transcendentals=0),
        **params,
    )(*args)


def fetch(sources, targets, sems):
    copies = [
        pltpu.make_async_copy(s, t, sems.at[i]) for i, (s, t) in enumerate(zip(sources, targets))
    ]
    for copy in copies:
        copy.start()
    for copy in copies:
        copy.wait()


def like(*args):
    return [pltpu.VMEM(a.shape, a.dtype) for a in args]


def pack_kernel(*refs):
    (atom_count, edge_count), far, (rows_o, edges_o) = refs[:2], refs[2:6], refs[6:8]
    near, sems = refs[8:12], refs[12]
    fetch(far, near, sems)
    positions, species, sender, receiver = near
    atoms, count = species.shape[-1], sender.shape[-1]
    owned = lax.broadcasted_iota(jnp.int32, (1, atoms), 1) < atom_count[0, 0, 0]
    kinds = jnp.where(owned, species[0, 0], -1).astype(F32)
    for c, part in enumerate([positions[k, 0, 0] for k in range(3)] + [kinds]):
        rows_o[0:1, atoms * c : atoms * c + atoms] = part
    rows_o[...] = jnp.broadcast_to(rows_o[0:1], rows_o.shape)
    live = lax.broadcasted_iota(jnp.int32, (1, count), 1) < edge_count[0, 0, 0]
    s, r = sender[0, 0], receiver[0, 0]
    edges_o[0:1] = jnp.where(live, s, 1023)
    edges_o[1:2] = jnp.where(live, r, 99)


def weights_kernel(*refs):
    far, outs, near, sems = refs[:9], refs[9:23], refs[23:28], refs[28]
    (emb_o, t0_o, win_o, wout_o, woutb_o, wup_o, mix_o, mixt_o, wupt_o, hw_o), kept = outs[:10], outs[10:]
    fetch(far, list(near) + list(kept), sems)
    embed, rin, rout, wup, wmix = near
    wupt_o[...] = rows3(wup[1].T)
    for t in range(2):
        mix_o[t] = rows3(wmix[t])
        mixt_o[t] = rows3(wmix[t].T)
    hw_o[...] = rows3(kept[2][...].T)
    emb_o[...] = jnp.zeros_like(emb_o)
    emb_o[0 : embed.shape[0]] = embed[...].astype(BF16).astype(F32)
    table = nn(emb_o[...], wup[0], precision=HIGH)
    hi, lo = split(table.T)
    t0_o[...] = jnp.concatenate([hi, lo], axis=1)
    for t in range(2):
        hi, lo = split(rin[t])
        hi, lo = hi.astype(F32), lo.astype(F32)
        both = jnp.concatenate([hi, hi, lo, jnp.zeros_like(hi)], axis=0)
        win_o[t] = both.T.astype(BF16)
        hi, lo = split(rout[t])
        woutb_o[t] = hi
        hi, lo = hi.astype(F32), lo.astype(F32)
        both = jnp.concatenate([hi, hi, lo], axis=0)
        wout_o[t] = both.T.astype(BF16)
    hi, lo = split(wup[1].T)
    wup_o[...] = jnp.concatenate([hi, lo], axis=1)


def pick_kernel(chosen, plane, out):
    out[...] = nn(chosen[...], plane[...], precision=HIGH)


def own_kernel(box, *refs):
    (below, level, above, edges), weights = refs[:4], refs[4:10]
    (mask_o, full_o, h1_o, parts, table), results = refs[10:15], refs[15:20]
    table[...] = jnp.zeros_like(table)
    for dy, near in enumerate((below, level, above)):
        for i in range(5):
            table[9 * i + 3 * dy : 9 * i + 3 * dy + 3] = near[3 * i : 3 * i + 3]
    rows = table[...]
    hi = rows.astype(BF16).astype(F32)
    rest = rows - hi
    mid = rest.astype(BF16).astype(F32)
    low = rest - mid
    for c in range(4):
        parts[c] = jnp.concatenate([p[:, 32 * c : 32 * c + 32] for p in (hi, mid, low)], axis=1)
    h1, mask = first_layer(box, 9, edges, *weights, *results, table, parts)
    h1_o[...] = h1.astype(BF16)
    full_o[...] = h1
    mask_o[...] = mask


def sides_kernel(box, before, after, parts, table, h1, *refs):
    weights, h1_o, results = refs[:6], refs[6], refs[7:]
    h1_o[32:64] = h1[...]
    for brick, edges in ((0, before), (2, after)):
        found = results[:5] if brick == 0 else results[5:]
        value, _ = first_layer(box, 9 * brick, edges, *weights, *found, table, parts)
        h1_o[32 * brick : 32 * brick + 32] = value.astype(BF16)


def first_layer(
    box, start, edges, emb, t0, win, wout, lam, mix, geo_o, pool_o, at_o, lift_o, base_o, table, parts
):
    lhs = jnp.concatenate([parts[c, start : start + 32] for c in range(4)], axis=0).astype(BF16)
    middle = start + 13
    mine = [parts[c, middle : middle + 1] for c in range(4)] + [jnp.zeros((4, 96), F32)]
    mine = jnp.concatenate(mine, axis=0)
    sender = edges[0:1]
    receiver = edges[1:2]
    slot = ones_at(jnp.bitwise_and(sender, 31), 32).astype(BF16)
    block = ones_at(jnp.right_shift(sender, 5), 32)
    recv = ones_at(receiver, 32)
    recv_b = recv.astype(BF16)
    got = nn(lhs, jnp.concatenate([slot] * 3, axis=0))
    at_recv = nn(mine.astype(BF16), jnp.concatenate([recv_b] * 3, axis=0))
    sent = [jnp.sum(got[32 * c : 32 * c + 32] * block, axis=0, keepdims=True) for c in range(4)]
    rel = []
    for c in range(3):
        d = sent[c] - at_recv[c : c + 1]
        d = d - jnp.round(d * (1.0 / box[c])) * box[c]
        rel.append(d * (1.0 / cutoff_radius))
    x, y, z = rel
    d2 = x * x + y * y + z * z
    reach = jnp.maximum(1.0 - d2, 0.0)
    env = reach * reach
    denv = -2.0 * reach
    geo_o[...] = jnp.concatenate([x, y, z, d2, env, denv, d2, d2], axis=0)
    harmonics = [
        jnp.ones_like(x),
        S3 * x,
        S3 * y,
        S3 * z,
        S15 * x * y,
        S15 * y * z,
        S15 * x * z,
        0.5 * S15 * (x * x - y * y),
        0.5 * S5 * (2.0 * z * z - x * x - y * y),
    ]
    for m, value in enumerate(harmonics):
        pool_o[32 * m : 32 * m + 32] = (recv * (value * 0.125)).astype(BF16)
    hidden, _ = hidden_units(d2, env, denv, win[0])
    radial = nn(wout[0], stack3(hidden))
    kind = ones_at(sent[3].astype(jnp.int32), 128).astype(BF16)
    lift = nn(t0[...], jnp.concatenate([kind, kind], axis=0))
    lift_o[...] = lift.astype(BF16)
    sums = []
    for order, (a, b) in enumerate(((0, 32), (32, 128), (128, 288))):
        base = (radial[128 * order : 128 * order + 128] * lift).astype(BF16)
        base_o[128 * order : 128 * order + 128] = base
        sums.append(nt(pool_o[a:b], base))
    product = sums[0]
    for order in (1, 2):
        total = sums[order]
        weight = lam[0, order - 1 : order]
        square = sum(
            total[32 * m : 32 * m + 32] * total[32 * m : 32 * m + 32]
            for m in range(2 * order + 1)
        )
        product = product + weight * square
        first = 0 if order == 1 else 96
        at_o[first : first + 32 * (2 * order + 1)] = (2.0 * weight * total).astype(BF16)
    kinds = table[middle : middle + 1, 96:128]
    mask = jnp.where(kinds >= 0.0, 1.0, 0.0)
    own_kind = jnp.where(
        lax.broadcasted_iota(jnp.int32, (128, 32), 0) == kinds.astype(jnp.int32), 1.0, 0.0
    ).astype(BF16)
    h0 = tn(own_kind, emb[...].astype(BF16))
    return h0 + product3(product, mix[0]), mask


def radial_kernel(
    edges, geo, win, wout, mask, h1, read_one, read_out, hot_o, rad_o, slope_o, e1_o, seed1_o, seed2_o
):
    s = edges[0:1]
    block, slot = jnp.right_shift(s, 5), jnp.bitwise_and(s, 31)
    one = lambda flag: jnp.where(flag, 1, 0)
    bx = one(block >= 9) + one(block >= 18)
    block = block - 9 * bx
    by = one(block >= 3) + one(block >= 6)
    bz = block - 3 * by
    s = (bz * 9 + by * 3 + bx) * 32 + slot
    sender = s
    for r in range(0, 864, 96):
        row = lax.broadcasted_iota(jnp.int32, (96, sender.shape[1]), 0) + r
        hot_o[r : r + 96] = jnp.where(row == sender, 1.0, 0.0).astype(BF16)
    hidden, slope = hidden_units(geo[3:4], geo[4:5], geo[5:6], win[1])
    rad_o[...] = nn(wout[1], stack3(hidden))
    slope_o[...] = slope
    e1_o[...] = nt(read_one[...], h1[...], precision=HIGH) * mask[...]
    mask8 = jnp.concatenate([mask[...], jnp.zeros((7, 32), F32)], axis=0)
    zero = lax.broadcasted_iota(jnp.int32, (8, 128), 0) == 0
    seed1_o[...] = tn(mask8, jnp.where(zero, read_one[...], 0.0), precision=HIGH)
    zero = lax.broadcasted_iota(jnp.int32, (8, 16), 0) == 0
    seed2_o[...] = tn(mask8, jnp.where(zero, read_out[...], 0.0), precision=HIGH)


def direction_kernel(edges, geo, pool, at, lift, base, win, wout, v_o):
    x, y, z = geo[0:1], geo[1:2], geo[2:3]
    recv = ones_at(edges[1:2], 32)
    _, slope = hidden_units(geo[3:4], geo[4:5], geo[5:6], win[0])
    drad = nn(wout[0], stack3(slope))
    g1 = tn(at[0:96], pool[32:128])
    g2 = tn(at[96:256], pool[128:288])
    common = drad[0:128] * 0.125 + drad[128:256] * g1 + drad[256:384] * g2
    common = lift[...].astype(F32) * common
    b1 = base[128:256].astype(F32)
    b2 = base[256:384].astype(F32)
    recv8 = recv * 0.125
    turns = (
        ((0, S15 * y), (2, S15 * z), (3, S15 * x), (4, -S5 * x)),
        ((0, S15 * x), (1, S15 * z), (3, -S15 * y), (4, -S5 * y)),
        ((1, S15 * y), (2, S15 * x), (4, 2.0 * S5 * z)),
    )
    for k, coordinate in enumerate((x, y, z)):
        h1 = tn(at[32 * k : 32 * k + 32], (recv8 * S3).astype(BF16))
        left = jnp.concatenate([at[96 + 32 * m : 128 + 32 * m] for m, _ in turns[k]], axis=0)
        right = jnp.concatenate([(recv8 * f).astype(BF16) for _, f in turns[k]], axis=0)
        h2 = tn(left, right)
        v = common * (2.0 * coordinate) + b1 * h1 + b2 * h2
        v_o[128 * k : 128 * k + 128] = v.astype(BF16)


def second_kernel(
    left, own, right, hotref, rad, pool, wup, lam, mix, mix_t, hidden_w, read_hidden, seed2,
    dleft_o, down_o, dright_o, dh2_o, e2_o, drad_o, base_o, da_o,
):
    feats = jnp.concatenate([left[...], own[...], right[...]], axis=0)
    got = tn(feats, hotref[...]).astype(BF16)
    lift = nn(wup[...], jnp.concatenate([got, got], axis=0))
    sums = []
    spans = ((0, 32), (32, 128), (128, 288))
    for order, (a, b) in enumerate(spans):
        base = (rad[128 * order : 128 * order + 128] * lift).astype(BF16)
        base_o[128 * order : 128 * order + 128] = base
        sums.append(nt(pool[a:b], base))
    product = sums[0]
    for order in (1, 2):
        total = sums[order]
        square = sum(
            total[32 * m : 32 * m + 32] * total[32 * m : 32 * m + 32]
            for m in range(2 * order + 1)
        )
        product = product + lam[1, order - 1 : order] * square
    h2 = own[128:160].astype(F32) + product3(product, mix[1])
    pre = product3(h2, hidden_w[...])
    sig = 1.0 / (1.0 + jnp.exp(-pre))
    inner = pre * sig
    seed = seed2[...]
    e2_o[...] = nt(jnp.ones((8, 16), F32), inner * seed, precision=HIGH)
    dpre = seed * sig * (1.0 + pre * (1.0 - sig))
    dh2 = nn(dpre, read_hidden[...], precision=HIGH)
    dh2_o[...] = dh2
    dp = product3(dh2, mix_t[1])
    da_o[0:32] = dp.astype(BF16)
    for order in (1, 2):
        weight = 2.0 * lam[1, order - 1 : order] * dp
        a = spans[order][0]
        for m in range(2 * order + 1):
            piece = weight * sums[order][32 * m : 32 * m + 32]
            da_o[a + 32 * m : a + 32 * m + 32] = piece.astype(BF16)
    dlift = None
    for order, (a, b) in enumerate(spans):
        g = tn(da_o[a:b], pool[a:b])
        drad_o[128 * order : 128 * order + 128] = (lift * g).astype(BF16)
        term = rad[128 * order : 128 * order + 128] * g
        dlift = term if dlift is None else dlift + term
    hi, lo = split(dlift)
    back = nt(hotref[...], jnp.concatenate([hi, lo], axis=0))
    back = back[:, 0:128] + back[:, 128:256]
    dleft_o[...] = back[0:288].astype(BF16)
    down_o[...] = back[288:576]
    dright_o[...] = back[576:864].astype(BF16)


def slope_kernel(edges, geo, slope, drad, base, da, woutb, drel_o):
    x, y, z = geo[0:1], geo[1:2], geo[2:3]
    recv8 = ones_at(edges[1:2], 32) * 0.125
    dhidden = nn(woutb[1], drad[...])
    dd2 = 2.0 * jnp.sum(dhidden * slope[...], axis=0, keepdims=True)
    q1 = nn(da[32:128], base[128:256])
    q2 = nn(da[128:288], base[256:384])
    one = [
        jnp.sum(q1[32 * m : 32 * m + 32] * recv8, axis=0, keepdims=True) * S3 for m in range(3)
    ]
    two = [jnp.sum(q2[32 * m : 32 * m + 32] * recv8, axis=0, keepdims=True) for m in range(5)]
    dx = dd2 * x + one[0] + S15 * (two[0] * y + two[2] * z + two[3] * x) - S5 * two[4] * x
    dy = dd2 * y + one[1] + S15 * (two[0] * x + two[1] * z - two[3] * y) - S5 * two[4] * y
    dz = dd2 * z + one[2] + S15 * (two[1] * y + two[2] * x) + 2.0 * S5 * two[4] * z
    none = jnp.zeros_like(dx)
    drel_o[...] = jnp.concatenate([dx, dy, dz, none, none, none, none, none], axis=0)


def force_kernel(*refs):
    edges_all, folded, (dh2, seed1, e1, e2, wup_t, mix_t), v_all = refs[:3], refs[3], refs[4:10], refs[10:13]
    drel2, outs, rows = refs[13], refs[14:17], refs[17]
    rows[...] = jnp.zeros_like(rows)
    dh1 = product3(folded[...], wup_t[...])
    dh1 = jnp.concatenate([dh1[0:32], dh1[32:64] + dh2[...] + seed1[...], dh1[64:96]], axis=0)
    dp = product3(dh1, mix_t[0])
    for brick in range(3):
        start = 9 * brick
        edges, v = edges_all[brick], v_all[brick]
        hi, lo = split(dp[32 * brick : 32 * brick + 32])
        dp2 = jnp.concatenate([hi, lo], axis=0)
        sender = edges[0:1]
        recv = ones_at(edges[1:2], 32)
        slot = ones_at(jnp.bitwise_and(sender, 31), 32).astype(BF16)
        block = ones_at(jnp.right_shift(sender, 5), 32)
        spread, pulled = [], []
        for k in range(3):
            q = nn(dp2, v[128 * k : 128 * k + 128])
            q = q[0:32] + q[32:64]
            drel = jnp.sum(q * recv, axis=0, keepdims=True)
            if brick == 1:
                drel = drel + drel2[k : k + 1]
            force = drel * (-1.0 / cutoff_radius)
            hi, lo = split(force)
            hi, lo = hi.astype(F32), lo.astype(F32)
            spread += [block * hi, block * lo]
            pulled += [hi, lo]
        pushed = nt(jnp.concatenate(spread, axis=0).astype(BF16), slot)
        pulled = jnp.concatenate(pulled + [jnp.zeros_like(hi)] * 2, axis=0).astype(BF16)
        pulled = nt(pulled, recv.astype(BF16))
        middle = start + 13
        for k in range(3):
            lanes = slice(32 * k, 32 * k + 32)
            rows[start : start + 27, lanes] += (
                pushed[64 * k : 64 * k + 27] + pushed[64 * k + 32 : 64 * k + 59]
            )
            rows[middle : middle + 1, lanes] -= pulled[2 * k : 2 * k + 1] + pulled[2 * k + 1 : 2 * k + 2]
    rows[22:23, 96:128] = e1[...] + e2[0:1]
    for dx in range(5):
        for dy, out in enumerate(outs):
            out[3 * dx : 3 * dx + 3] = rows[9 * dx + 3 * dy : 9 * dx + 3 * dy + 3]
    for out in outs:
        out[15:16] = jnp.zeros((1, 128), F32)


def spread_kernel(chosen, a, b, c, out):
    out[...] = tn(chosen[...], a[...] + b[...] + c[...], precision=HIGH)


def last_kernel(rows, energy_o, forces_o):
    atoms = energy_o.shape[-1]
    total = jnp.sum(rows[...], axis=0, keepdims=True)
    energy_o[0, 0] = total[:, 3 * atoms : 4 * atoms]
    for k in range(3):
        forces_o[k, 0, 0] = total[:, atoms * k : atoms * k + atoms]


def local(
    positions, species, atom_count, edge_count, sender, receiver, image_shift,
    embed, radial_in, radial_out, w_up, lam, w_mix, read_one, read_hidden, read_out,
):
    atoms = positions.shape[-1]
    count = sender.shape[-1]
    box = (SIDE * 4 * lattice_step, SIDE * 4 * lattice_step, SIDE * (atoms // 16) * lattice_step)

    chosen = around()
    rows, edges = call(
        pack_kernel, [((SIDE * SIDE, 4 * atoms), F32), ((2, count), jnp.int32)],
        atom_count, edge_count, positions, species, sender, receiver, far=True,
        scratch=like(positions, species, sender, receiver),
    )
    edges = move(edges, bring_home())
    level = exchange(rows)

    weights = call(
        weights_kernel,
        [((128, 128), F32), ((128, 256), BF16), ((2, 64, 32), BF16), ((2, 384, 192), BF16),
         ((2, 64, 384), BF16), ((128, 256), BF16), ((2, 384, 128), BF16), ((2, 384, 128), BF16), ((384, 128), BF16),
         ((384, 16), BF16), ((2, 2, 128), F32), ((1, 128), F32), ((16, 128), F32), ((1, 16), F32)],
        embed, radial_in, radial_out, w_up, w_mix, lam, read_one[None], read_hidden.T, read_out[None],
        far=True, scratch=like(embed, radial_in, radial_out, w_up, w_mix),
    )
    level, weights = lax.optimization_barrier((level, weights))
    (level,) = call(pick_kernel, [((16, 128), F32)], chosen, level)
    emb, t0, win, wout, woutb, wup, mix, mix_t, wup_t, hidden_w, lam, read_one, read_hidden, read_out = weights
    below, level, above = widen(level, 1)
    edges, above = lax.optimization_barrier((edges, above))
    both = edges[0:1] + edges[1:2] * 65536
    edges = [
        e if k == 1 else jnp.concatenate([jnp.bitwise_and(e, 65535), jnp.right_shift(e, 16)], axis=0)
        for k, e in enumerate((move(both, shift(0, -1)), edges, move(both, shift(0, 1))))
    ]

    results = [((8, count), F32), ((288, count), BF16), ((256, 128), BF16), ((128, count), BF16),
               ((384, count), BF16)]
    mask, h1_full, h1, parts, table, *own = call(
        functools.partial(own_kernel, box),
        [((1, 32), F32), ((32, 128), F32), ((32, 128), BF16), ((4, 56, 96), F32), ((56, 128), F32)]
        + results,
        below, level, above, edges[1], emb, t0, win, wout, lam, mix,
    )
    h1, *sides = call(
        functools.partial(sides_kernel, box), [((96, 128), BF16)] + results * 2,
        edges[0], edges[2], parts, table, h1, emb, t0, win, wout, lam, mix,
    )
    per_brick = (sides[:5], own, sides[5:])
    geo, pool = per_brick[1][:2]

    def direction(brick, found=None):
        found = per_brick[brick] if found is None else found
        return call(
            direction_kernel, [((384, count), BF16)], edges[brick], *found, win, wout,
            flops=1_000_000_000,
        )[0]

    hidden = call(
        radial_kernel,
        [((864, count), BF16), ((384, count), F32), ((64, count), F32), ((1, 32), F32), ((32, 128), F32),
         ((32, 16), F32)],
        edges[1], geo, win, wout, mask, h1_full, read_one, read_out, flops=1_000_000_000,
    )
    plane = jnp.concatenate(widen(h1, 1), axis=0)
    plane, (hotref, rad, slope, e1, seed1, seed2) = lax.optimization_barrier((plane, hidden))
    left, own, right = widen(plane, 2)
    left, right, v_own = lax.optimization_barrier((left, right, direction(1)))

    dleft, down, dright, dh2, e2, drad, base2, da = call(
        second_kernel,
        [((288, 128), BF16), ((288, 128), F32), ((288, 128), BF16), ((32, 128), F32), ((8, 32), F32),
         ((384, count), BF16), ((384, count), BF16), ((288, 128), BF16)],
        left, own, right, hotref, rad, pool, wup, lam, mix, mix_t, hidden_w, read_hidden, seed2,
    )
    dh2, before = lax.optimization_barrier((dh2, per_brick[0]))
    v_before = direction(0, before)

    plane = down + move(dleft, shift(2, 1)).astype(F32) + move(dright, shift(2, -1)).astype(F32)
    plane, v_before, after = lax.optimization_barrier((plane, v_before, per_brick[2]))
    v_after = direction(2, after)
    folded = (
        plane[96:192]
        + move(plane[0:96].astype(BF16), shift(1, 1)).astype(F32)
        + move(plane[192:288].astype(BF16), shift(1, -1)).astype(F32)
    )

    (drel2,) = call(
        slope_kernel, [((8, count), F32)], edges[1], geo, slope, drad, base2, da, woutb,
        flops=1_000_000_000,
    )

    below, level, above = call(
        force_kernel, [((16, 128), F32)] * 3,
        *edges, folded, dh2, seed1, e1, e2, wup_t, mix_t, v_before, v_own, v_after, drel2,
        scratch=[pltpu.VMEM((48, 128), F32)],
    )

    (rows,) = call(
        spread_kernel, [((SIDE * SIDE, 4 * atoms), F32)],
        chosen, level, move(below, shift(1, 1)), move(above, shift(1, -1)),
    )
    return call(
        last_kernel, [((1, 1, 1, atoms), F32), ((3, 1, 1, 1, atoms), F32)], exchange(rows)
    )


def solution(mesh):
    cell = P("gx", "gy", "gz")
    in_specs = (
        P(None, "gx", "gy", "gz", None),
        P("gx", "gy", "gz", None),
        cell,
        cell,
        P("gx", "gy", "gz", None),
        P("gx", "gy", "gz", None),
        P(None, "gx", "gy", "gz", None),
    ) + (P(),) * 9
    out_specs = (P("gx", "gy", "gz", None), P(None, "gx", "gy", "gz", None))
    return jax.shard_map(local, mesh=mesh, in_specs=in_specs, out_specs=out_specs, check_vma=False)
```

```python
import functools

import jax
import jax.numpy as jnp
import numpy as np
from jax import lax
from jax.experimental import pallas as pl
from jax.experimental.pallas import tpu as pltpu
from jax.sharding import PartitionSpec as P

cutoff_radius = 5.0
lattice_step = 2.25
AXES = ("gx", "gy", "gz")
SIDE = 8
F32 = jnp.float32
BF16 = jnp.bfloat16
S3 = 3.0**0.5
S5 = 5.0**0.5
S15 = 15.0**0.5
HIGH = lax.Precision.HIGHEST


def place(a, b, d):
    return (a * SIDE + b) * SIDE + d


def home(a, b, d):
    return place((a % 4) * 2 + d % 2, b, (d // 2) * 2 + a // 4)


def bricks():
    return [(a, b, d) for a in range(SIDE) for b in range(SIDE) for d in range(SIDE)]


def move(x, pairs):
    return lax.ppermute(x, AXES, pairs)


def bring_home():
    return [(place(a, b, d), home(a, b, d)) for a, b, d in bricks()]


def around():
    gx, gz = lax.axis_index("gx"), lax.axis_index("gz")
    a, d = (gz % 2) * 4 + gx // 2, (gz // 2) * 2 + gx % 2
    k = lax.broadcasted_iota(jnp.int32, (16, SIDE * SIDE), 0)
    at = lax.broadcasted_iota(jnp.int32, (16, SIDE * SIDE), 1)
    i = k // 3
    place_k = ((a + i + SIDE - 2) % SIDE) * SIDE + (d + k - 3 * i + SIDE - 1) % SIDE
    return jnp.where((place_k == at) & (k < 15), 1.0, 0.0).astype(F32)


def exchange(x):
    rows = x.reshape(x.shape[0], 1, x.shape[1])
    return lax.all_to_all(rows, ("gx", "gz"), 0, 0, tiled=True).reshape(x.shape)


def shift(axis, step):
    pairs = []
    for cell in bricks():
        other = list(cell)
        other[axis] = (other[axis] + step) % SIDE
        pairs.append((home(*other), home(*cell)))
    return pairs


def widen(x, axis):
    return [move(x, shift(axis, -1)), x, move(x, shift(axis, 1))]


def nn(a, b, **kw):
    return lax.dot_general(a, b, (((1,), (0,)), ((), ())), preferred_element_type=F32, **kw)


def nt(a, b, **kw):
    return lax.dot_general(a, b, (((1,), (1,)), ((), ())), preferred_element_type=F32, **kw)


def tn(a, b, **kw):
    return lax.dot_general(a, b, (((0,), (0,)), ((), ())), preferred_element_type=F32, **kw)


def split(x):
    hi = x.astype(BF16)
    return hi, (x - hi.astype(F32)).astype(BF16)


def stack3(x):
    hi, lo = split(x)
    return jnp.concatenate([hi, lo, hi], axis=0)


def product3(x, stack):
    hi, lo = split(x)
    return nn(jnp.concatenate([hi, lo, hi], axis=1), stack)


def rows3(w):
    hi, lo = split(w)
    return jnp.concatenate([hi, hi, lo], axis=0)


def hot(index, rows):
    edges = index.shape[1]
    return lax.broadcasted_iota(jnp.int32, (rows, edges), 0) == index


def ones_at(index, rows):
    return jnp.where(hot(index, rows), 1.0, 0.0).astype(F32)


def small_stack(x):
    hi, lo = split(x)
    hi, lo = hi.astype(F32), lo.astype(F32)
    return jnp.concatenate([hi, lo, hi, jnp.zeros_like(x)], axis=0).astype(BF16)


def hidden_units(d2, env, denv, win):
    edges = d2.shape[1]
    centre = lax.broadcasted_iota(jnp.int32, (8, edges), 0).astype(F32) * (1.0 / 7.0)
    gap = d2 - centre
    basis = jnp.exp(-64.0 * gap * gap)
    pre = nn(win, small_stack(basis))
    if denv is None:
        return pre / (1.0 + jnp.exp(-pre)) * env, None
    slope = basis * (-128.0 * gap)
    dpre = nn(win, small_stack(slope))
    sig = 1.0 / (1.0 + jnp.exp(-pre))
    act = pre * sig
    dact = sig * (1.0 + pre * (1.0 - sig)) * dpre
    return act * env, dact * env + act * denv


def call(kernel, outs, *args, flops=1_000_000, limit=16, scratch=(), far=False):
    params = {}
    if far:
        spaces = [pltpu.SMEM if a.size == 1 else pltpu.HBM for a in args]
        args = [
            a if s is pltpu.SMEM else pltpu.with_memory_space_constraint(a, s)
            for a, s in zip(args, spaces)
        ]
        params["in_specs"] = [pl.BlockSpec(memory_space=s) for s in spaces]
        scratch = list(scratch) + [pltpu.SemaphoreType.DMA((len(args),))]
    return pl.pallas_call(
        kernel,
        out_shape=tuple(jax.ShapeDtypeStruct(s, d) for s, d in outs),
        scratch_shapes=scratch,
        compiler_params=pltpu.CompilerParams(vmem_limit_bytes=limit * 1024 * 1024),
        cost_estimate=pl.CostEstimate(flops=flops, bytes_accessed=1_000_000, transcendentals=0),
        **params,
    )(*args)


def fetch(sources, targets, sems):
    copies = [
        pltpu.make_async_copy(s, t, sems.at[i]) for i, (s, t) in enumerate(zip(sources, targets))
    ]
    for copy in copies:
        copy.start()
    for copy in copies:
        copy.wait()


def like(*args):
    return [pltpu.VMEM(a.shape, a.dtype) for a in args]


def pack_kernel(*refs):
    (atom_count, edge_count), far, (rows_o, edges_o) = refs[:2], refs[2:6], refs[6:8]
    near, sems = refs[8:12], refs[12]
    fetch(far, near, sems)
    positions, species, sender, receiver = near
    atoms, count = species.shape[-1], sender.shape[-1]
    owned = lax.broadcasted_iota(jnp.int32, (1, atoms), 1) < atom_count[0, 0, 0]
    kinds = jnp.where(owned, species[0, 0], -1).astype(F32)
    for c, part in enumerate([positions[k, 0, 0] for k in range(3)] + [kinds]):
        rows_o[0:1, atoms * c : atoms * c + atoms] = part
    rows_o[...] = jnp.broadcast_to(rows_o[0:1], rows_o.shape)
    live = lax.broadcasted_iota(jnp.int32, (1, count), 1) < edge_count[0, 0, 0]
    s, r = sender[0, 0], receiver[0, 0]
    edges_o[0:1] = jnp.where(live, s, 1023)
    edges_o[1:2] = jnp.where(live, r, 99)


def weights_kernel(*refs):
    far, outs, near, sems = refs[:9], refs[9:23], refs[23:28], refs[28]
    (emb_o, t0_o, win_o, wout_o, woutb_o, wup_o, mix_o, mixt_o, wupt_o, hw_o), kept = outs[:10], outs[10:]
    fetch(far, list(near) + list(kept), sems)
    embed, rin, rout, wup, wmix = near
    wupt_o[...] = rows3(wup[1].T)
    for t in range(2):
        mix_o[t] = rows3(wmix[t])
        mixt_o[t] = rows3(wmix[t].T)
    hw_o[...] = rows3(kept[2][...].T)
    emb_o[...] = jnp.zeros_like(emb_o)
    emb_o[0 : embed.shape[0]] = embed[...].astype(BF16).astype(F32)
    table = nn(emb_o[...], wup[0], precision=HIGH)
    hi, lo = split(table.T)
    t0_o[...] = jnp.concatenate([hi, lo], axis=1)
    for t in range(2):
        hi, lo = split(rin[t])
        hi, lo = hi.astype(F32), lo.astype(F32)
        both = jnp.concatenate([hi, hi, lo, jnp.zeros_like(hi)], axis=0)
        win_o[t] = both.T.astype(BF16)
        hi, lo = split(rout[t])
        woutb_o[t] = hi
        hi, lo = hi.astype(F32), lo.astype(F32)
        both = jnp.concatenate([hi, hi, lo], axis=0)
        wout_o[t] = both.T.astype(BF16)
    hi, lo = split(wup[1].T)
    wup_o[...] = jnp.concatenate([hi, lo], axis=1)


def pick_kernel(chosen, plane, out):
    out[...] = nn(chosen[...], plane[...], precision=HIGH)


def own_kernel(box, *refs):
    (below, level, above, edges), weights = refs[:4], refs[4:10]
    (mask_o, full_o, h1_o, parts, table), results = refs[10:15], refs[15:20]
    table[...] = jnp.zeros_like(table)
    for dy, near in enumerate((below, level, above)):
        for i in range(5):
            table[9 * i + 3 * dy : 9 * i + 3 * dy + 3] = near[3 * i : 3 * i + 3]
    rows = table[...]
    hi = rows.astype(BF16).astype(F32)
    rest = rows - hi
    mid = rest.astype(BF16).astype(F32)
    low = rest - mid
    for c in range(4):
        parts[c] = jnp.concatenate([p[:, 32 * c : 32 * c + 32] for p in (hi, mid, low)], axis=1)
    h1, mask = first_layer(box, 9, edges, *weights, *results, table, parts)
    h1_o[...] = h1.astype(BF16)
    full_o[...] = h1
    mask_o[...] = mask


def sides_kernel(box, before, after, parts, table, h1, *refs):
    weights, h1_o, results = refs[:6], refs[6], refs[7:]
    h1_o[32:64] = h1[...]
    for brick, edges in ((0, before), (2, after)):
        found = results[:5] if brick == 0 else results[5:]
        value, _ = first_layer(box, 9 * brick, edges, *weights, *found, table, parts)
        h1_o[32 * brick : 32 * brick + 32] = value.astype(BF16)


def first_layer(
    box, start, edges, emb, t0, win, wout, lam, mix, geo_o, pool_o, at_o, lift_o, base_o, table, parts
):
    lhs = jnp.concatenate([parts[c, start : start + 32] for c in range(4)], axis=0)
    middle = start + 13
    mine = [parts[c, middle : middle + 1] for c in range(4)] + [jnp.zeros((4, 96), F32)]
    mine = jnp.concatenate(mine, axis=0)
    sender = edges[0:1]
    receiver = edges[1:2]
    slot = ones_at(jnp.bitwise_and(sender, 31), 32).astype(BF16)
    block = ones_at(jnp.right_shift(sender, 5), 32)
    recv = ones_at(receiver, 32)
    recv_b = recv.astype(BF16)
    lhs = jnp.concatenate([lhs, jnp.zeros((128, 96), F32)], axis=1)
    mine = jnp.concatenate([jnp.zeros((8, 96), F32), mine], axis=1)
    got = nn(
        jnp.concatenate([lhs, mine], axis=0).astype(BF16),
        jnp.concatenate([slot] * 3 + [recv_b] * 3, axis=0),
    )
    at_recv = got[128:136]
    sent = [jnp.sum(got[32 * c : 32 * c + 32] * block, axis=0, keepdims=True) for c in range(4)]
    rel = []
    for c in range(3):
        d = sent[c] - at_recv[c : c + 1]
        d = d - jnp.round(d * (1.0 / box[c])) * box[c]
        rel.append(d * (1.0 / cutoff_radius))
    x, y, z = rel
    d2 = x * x + y * y + z * z
    reach = jnp.maximum(1.0 - d2, 0.0)
    env = reach * reach
    denv = -2.0 * reach
    geo_o[...] = jnp.concatenate([x, y, z, d2, env, denv, d2, d2], axis=0)
    harmonics = [
        jnp.ones_like(x),
        S3 * x,
        S3 * y,
        S3 * z,
        S15 * x * y,
        S15 * y * z,
        S15 * x * z,
        0.5 * S15 * (x * x - y * y),
        0.5 * S5 * (2.0 * z * z - x * x - y * y),
    ]
    for m, value in enumerate(harmonics):
        pool_o[32 * m : 32 * m + 32] = (recv * (value * 0.125)).astype(BF16)
    hidden, _ = hidden_units(d2, env, None, win[0])
    radial = nn(wout[0], stack3(hidden))
    kind = ones_at(sent[3].astype(jnp.int32), 128).astype(BF16)
    lift = nn(t0[...], jnp.concatenate([kind, kind], axis=0))
    lift_o[...] = lift.astype(BF16)
    sums = []
    for order, (a, b) in enumerate(((0, 32), (32, 128), (128, 288))):
        base = (radial[128 * order : 128 * order + 128] * lift).astype(BF16)
        base_o[128 * order : 128 * order + 128] = base
        sums.append(nt(pool_o[a:b], base))
    product = sums[0]
    for order in (1, 2):
        total = sums[order]
        weight = lam[0, order - 1 : order]
        square = sum(
            total[32 * m : 32 * m + 32] * total[32 * m : 32 * m + 32]
            for m in range(2 * order + 1)
        )
        product = product + weight * square
        first = 0 if order == 1 else 96
        at_o[first : first + 32 * (2 * order + 1)] = (2.0 * weight * total).astype(BF16)
    kinds = table[middle : middle + 1, 96:128]
    mask = jnp.where(kinds >= 0.0, 1.0, 0.0)
    own_kind = jnp.where(
        lax.broadcasted_iota(jnp.int32, (128, 32), 0) == kinds.astype(jnp.int32), 1.0, 0.0
    ).astype(BF16)
    h0 = tn(own_kind, emb[...].astype(BF16))
    return h0 + product3(product, mix[0]), mask


def radial_kernel(
    edges, geo, win, wout, mask, h1, read_one, read_out, hot_o, rad_o, slope_o, e1_o, seed1_o, seed2_o
):
    s = edges[0:1]
    block, slot = jnp.right_shift(s, 5), jnp.bitwise_and(s, 31)
    one = lambda flag: jnp.where(flag, 1, 0)
    bx = one(block >= 9) + one(block >= 18)
    block = block - 9 * bx
    by = one(block >= 3) + one(block >= 6)
    bz = block - 3 * by
    s = (bz * 9 + by * 3 + bx) * 32 + slot
    sender = s
    for r in range(0, 864, 96):
        row = lax.broadcasted_iota(jnp.int32, (96, sender.shape[1]), 0) + r
        hot_o[r : r + 96] = jnp.where(row == sender, 1.0, 0.0).astype(BF16)
    hidden, slope = hidden_units(geo[3:4], geo[4:5], geo[5:6], win[1])
    rad_o[...] = nn(wout[1], stack3(hidden))
    slope_o[...] = slope
    e1_o[...] = nt(read_one[...], h1[...], precision=HIGH) * mask[...]
    mask8 = jnp.concatenate([mask[...], jnp.zeros((7, 32), F32)], axis=0)
    zero = lax.broadcasted_iota(jnp.int32, (8, 128), 0) == 0
    seed1_o[...] = tn(mask8, jnp.where(zero, read_one[...], 0.0), precision=HIGH)
    zero = lax.broadcasted_iota(jnp.int32, (8, 16), 0) == 0
    seed2_o[...] = tn(mask8, jnp.where(zero, read_out[...], 0.0), precision=HIGH)


def direction_kernel(edges, geo, pool, at, lift, base, win, wout, v_o):
    x, y, z = geo[0:1], geo[1:2], geo[2:3]
    recv = ones_at(edges[1:2], 32)
    _, slope = hidden_units(geo[3:4], geo[4:5], geo[5:6], win[0])
    drad = nn(wout[0], stack3(slope))
    g1 = tn(at[0:96], pool[32:128])
    g2 = tn(at[96:256], pool[128:288])
    common = drad[0:128] * 0.125 + drad[128:256] * g1 + drad[256:384] * g2
    common = lift[...].astype(F32) * common
    b1 = base[128:256].astype(F32)
    b2 = base[256:384].astype(F32)
    recv8 = recv * 0.125
    turns = (
        ((0, S15 * y), (2, S15 * z), (3, S15 * x), (4, -S5 * x)),
        ((0, S15 * x), (1, S15 * z), (3, -S15 * y), (4, -S5 * y)),
        ((1, S15 * y), (2, S15 * x), (4, 2.0 * S5 * z)),
    )
    for k, coordinate in enumerate((x, y, z)):
        h1 = tn(at[32 * k : 32 * k + 32], (recv8 * S3).astype(BF16))
        left = jnp.concatenate([at[96 + 32 * m : 128 + 32 * m] for m, _ in turns[k]], axis=0)
        right = jnp.concatenate([(recv8 * f).astype(BF16) for _, f in turns[k]], axis=0)
        h2 = tn(left, right)
        v = common * (2.0 * coordinate) + b1 * h1 + b2 * h2
        v_o[128 * k : 128 * k + 128] = v.astype(BF16)


def second_kernel(
    left, own, right, hotref, rad, pool, wup, lam, mix, mix_t, hidden_w, read_hidden, seed2,
    dleft_o, down_o, dright_o, dh2_o, e2_o, drad_o, base_o, da_o,
):
    feats = jnp.concatenate([left[...], own[...], right[...]], axis=0)
    got = tn(feats, hotref[...]).astype(BF16)
    lift = nn(wup[...], jnp.concatenate([got, got], axis=0))
    sums = []
    spans = ((0, 32), (32, 128), (128, 288))
    for order, (a, b) in enumerate(spans):
        base = (rad[128 * order : 128 * order + 128] * lift).astype(BF16)
        base_o[128 * order : 128 * order + 128] = base
        sums.append(nt(pool[a:b], base))
    product = sums[0]
    for order in (1, 2):
        total = sums[order]
        square = sum(
            total[32 * m : 32 * m + 32] * total[32 * m : 32 * m + 32]
            for m in range(2 * order + 1)
        )
        product = product + lam[1, order - 1 : order] * square
    h2 = own[128:160].astype(F32) + product3(product, mix[1])
    pre = product3(h2, hidden_w[...])
    sig = 1.0 / (1.0 + jnp.exp(-pre))
    inner = pre * sig
    seed = seed2[...]
    e2_o[...] = nt(jnp.ones((8, 16), F32), inner * seed, precision=HIGH)
    dpre = seed * sig * (1.0 + pre * (1.0 - sig))
    dh2 = nn(dpre, read_hidden[...], precision=HIGH)
    dh2_o[...] = dh2
    dp = product3(dh2, mix_t[1])
    da_o[0:32] = dp.astype(BF16)
    for order in (1, 2):
        weight = 2.0 * lam[1, order - 1 : order] * dp
        a = spans[order][0]
        for m in range(2 * order + 1):
            piece = weight * sums[order][32 * m : 32 * m + 32]
            da_o[a + 32 * m : a + 32 * m + 32] = piece.astype(BF16)
    dlift = None
    for order, (a, b) in enumerate(spans):
        g = tn(da_o[a:b], pool[a:b])
        drad_o[128 * order : 128 * order + 128] = (lift * g).astype(BF16)
        term = rad[128 * order : 128 * order + 128] * g
        dlift = term if dlift is None else dlift + term
    hi, lo = split(dlift)
    back = nt(hotref[...], jnp.concatenate([hi, lo], axis=0))
    back = back[:, 0:128] + back[:, 128:256]
    dleft_o[...] = back[0:288].astype(BF16)
    down_o[...] = back[288:576]
    dright_o[...] = back[576:864].astype(BF16)


def slope_kernel(edges, geo, slope, drad, base, da, woutb, drel_o):
    x, y, z = geo[0:1], geo[1:2], geo[2:3]
    recv8 = ones_at(edges[1:2], 32) * 0.125
    dhidden = nn(woutb[1], drad[...])
    dd2 = 2.0 * jnp.sum(dhidden * slope[...], axis=0, keepdims=True)
    q1 = nn(da[32:128], base[128:256])
    q2 = nn(da[128:288], base[256:384])
    one = [
        jnp.sum(q1[32 * m : 32 * m + 32] * recv8, axis=0, keepdims=True) * S3 for m in range(3)
    ]
    two = [jnp.sum(q2[32 * m : 32 * m + 32] * recv8, axis=0, keepdims=True) for m in range(5)]
    dx = dd2 * x + one[0] + S15 * (two[0] * y + two[2] * z + two[3] * x) - S5 * two[4] * x
    dy = dd2 * y + one[1] + S15 * (two[0] * x + two[1] * z - two[3] * y) - S5 * two[4] * y
    dz = dd2 * z + one[2] + S15 * (two[1] * y + two[2] * x) + 2.0 * S5 * two[4] * z
    none = jnp.zeros_like(dx)
    drel_o[...] = jnp.concatenate([dx, dy, dz, none, none, none, none, none], axis=0)


def force_kernel(*refs):
    edges_all, folded, (dh2, seed1, e1, e2, wup_t, mix_t), v_all = refs[:3], refs[3], refs[4:10], refs[10:13]
    drel2, outs, rows = refs[13], refs[14:17], refs[17]
    rows[...] = jnp.zeros_like(rows)
    dh1 = product3(folded[...], wup_t[...])
    dh1 = jnp.concatenate([dh1[0:32], dh1[32:64] + dh2[...] + seed1[...], dh1[64:96]], axis=0)
    dp = product3(dh1, mix_t[0])
    for brick in range(3):
        start = 9 * brick
        edges, v = edges_all[brick], v_all[brick]
        hi, lo = split(dp[32 * brick : 32 * brick + 32])
        dp2 = jnp.concatenate([hi, lo], axis=0)
        sender = edges[0:1]
        recv = ones_at(edges[1:2], 32)
        slot = ones_at(jnp.bitwise_and(sender, 31), 32).astype(BF16)
        block = ones_at(jnp.right_shift(sender, 5), 32)
        spread, pulled = [], []
        for k in range(3):
            q = nn(dp2, v[128 * k : 128 * k + 128])
            q = q[0:32] + q[32:64]
            drel = jnp.sum(q * recv, axis=0, keepdims=True)
            if brick == 1:
                drel = drel + drel2[k : k + 1]
            force = drel * (-1.0 / cutoff_radius)
            hi, lo = split(force)
            hi, lo = hi.astype(F32), lo.astype(F32)
            spread += [block * hi, block * lo]
            pulled += [hi, lo]
        pushed = nt(jnp.concatenate(spread, axis=0).astype(BF16), slot)
        pulled = jnp.concatenate(pulled + [jnp.zeros_like(hi)] * 2, axis=0).astype(BF16)
        pulled = nt(pulled, recv.astype(BF16))
        middle = start + 13
        for k in range(3):
            lanes = slice(32 * k, 32 * k + 32)
            rows[start : start + 27, lanes] += (
                pushed[64 * k : 64 * k + 27] + pushed[64 * k + 32 : 64 * k + 59]
            )
            rows[middle : middle + 1, lanes] -= pulled[2 * k : 2 * k + 1] + pulled[2 * k + 1 : 2 * k + 2]
    rows[22:23, 96:128] = e1[...] + e2[0:1]
    for dx in range(5):
        for dy, out in enumerate(outs):
            out[3 * dx : 3 * dx + 3] = rows[9 * dx + 3 * dy : 9 * dx + 3 * dy + 3]
    for out in outs:
        out[15:16] = jnp.zeros((1, 128), F32)


def spread_kernel(chosen, a, b, c, out):
    out[...] = tn(chosen[...], a[...] + b[...] + c[...], precision=HIGH)


def last_kernel(rows, energy_o, forces_o):
    atoms = energy_o.shape[-1]
    total = jnp.sum(rows[...], axis=0, keepdims=True)
    energy_o[0, 0] = total[:, 3 * atoms : 4 * atoms]
    for k in range(3):
        forces_o[k, 0, 0] = total[:, atoms * k : atoms * k + atoms]


def local(
    positions, species, atom_count, edge_count, sender, receiver, image_shift,
    embed, radial_in, radial_out, w_up, lam, w_mix, read_one, read_hidden, read_out,
):
    atoms = positions.shape[-1]
    count = sender.shape[-1]
    box = (SIDE * 4 * lattice_step, SIDE * 4 * lattice_step, SIDE * (atoms // 16) * lattice_step)

    chosen = around()
    rows, edges = call(
        pack_kernel, [((SIDE * SIDE, 4 * atoms), F32), ((2, count), jnp.int32)],
        atom_count, edge_count, positions, species, sender, receiver, far=True,
        scratch=like(positions, species, sender, receiver),
    )
    edges = move(edges, bring_home())
    level = exchange(rows)

    weights = call(
        weights_kernel,
        [((128, 128), F32), ((128, 256), BF16), ((2, 64, 32), BF16), ((2, 384, 192), BF16),
         ((2, 64, 384), BF16), ((128, 256), BF16), ((2, 384, 128), BF16), ((2, 384, 128), BF16), ((384, 128), BF16),
         ((384, 16), BF16), ((2, 2, 128), F32), ((1, 128), F32), ((16, 128), F32), ((1, 16), F32)],
        embed, radial_in, radial_out, w_up, w_mix, lam, read_one[None], read_hidden.T, read_out[None],
        far=True, scratch=like(embed, radial_in, radial_out, w_up, w_mix),
    )
    level, weights = lax.optimization_barrier((level, weights))
    (level,) = call(pick_kernel, [((16, 128), F32)], chosen, level)
    emb, t0, win, wout, woutb, wup, mix, mix_t, wup_t, hidden_w, lam, read_one, read_hidden, read_out = weights
    below, level, above = widen(level, 1)
    edges, above = lax.optimization_barrier((edges, above))
    both = edges[0:1] + edges[1:2] * 65536
    edges = [
        e if k == 1 else jnp.concatenate([jnp.bitwise_and(e, 65535), jnp.right_shift(e, 16)], axis=0)
        for k, e in enumerate((move(both, shift(0, -1)), edges, move(both, shift(0, 1))))
    ]

    results = [((8, count), F32), ((288, count), BF16), ((256, 128), BF16), ((128, count), BF16),
               ((384, count), BF16)]
    mask, h1_full, h1, parts, table, *own = call(
        functools.partial(own_kernel, box),
        [((1, 32), F32), ((32, 128), F32), ((32, 128), BF16), ((4, 56, 96), F32), ((56, 128), F32)]
        + results,
        below, level, above, edges[1], emb, t0, win, wout, lam, mix,
    )
    h1, *sides = call(
        functools.partial(sides_kernel, box), [((96, 128), BF16)] + results * 2,
        edges[0], edges[2], parts, table, h1, emb, t0, win, wout, lam, mix,
    )
    per_brick = (sides[:5], own, sides[5:])
    geo, pool = per_brick[1][:2]

    def direction(brick, found=None):
        found = per_brick[brick] if found is None else found
        return call(
            direction_kernel, [((384, count), BF16)], edges[brick], *found, win, wout,
            flops=1_000_000_000,
        )[0]

    hidden = call(
        radial_kernel,
        [((864, count), BF16), ((384, count), F32), ((64, count), F32), ((1, 32), F32), ((32, 128), F32),
         ((32, 16), F32)],
        edges[1], geo, win, wout, mask, h1_full, read_one, read_out, flops=1_000_000_000,
    )
    plane = jnp.concatenate(widen(h1, 1), axis=0)
    plane, (hotref, rad, slope, e1, seed1, seed2) = lax.optimization_barrier((plane, hidden))
    left, own, right = widen(plane, 2)
    left, right, v_own = lax.optimization_barrier((left, right, direction(1)))

    dleft, down, dright, dh2, e2, drad, base2, da = call(
        second_kernel,
        [((288, 128), BF16), ((288, 128), F32), ((288, 128), BF16), ((32, 128), F32), ((8, 32), F32),
         ((384, count), BF16), ((384, count), BF16), ((288, 128), BF16)],
        left, own, right, hotref, rad, pool, wup, lam, mix, mix_t, hidden_w, read_hidden, seed2,
    )
    dh2, before = lax.optimization_barrier((dh2, per_brick[0]))
    v_before = direction(0, before)

    plane = down + move(dleft, shift(2, 1)).astype(F32) + move(dright, shift(2, -1)).astype(F32)
    plane, v_before, after = lax.optimization_barrier((plane, v_before, per_brick[2]))
    v_after = direction(2, after)
    folded = (
        plane[96:192]
        + move(plane[0:96].astype(BF16), shift(1, 1)).astype(F32)
        + move(plane[192:288].astype(BF16), shift(1, -1)).astype(F32)
    )

    (drel2,) = call(
        slope_kernel, [((8, count), F32)], edges[1], geo, slope, drad, base2, da, woutb,
        flops=1_000_000_000,
    )

    below, level, above = call(
        force_kernel, [((16, 128), F32)] * 3,
        *edges, folded, dh2, seed1, e1, e2, wup_t, mix_t, v_before, v_own, v_after, drel2,
        scratch=[pltpu.VMEM((48, 128), F32)],
    )

    (rows,) = call(
        spread_kernel, [((SIDE * SIDE, 4 * atoms), F32)],
        chosen, level, move(below, shift(1, 1)), move(above, shift(1, -1)),
    )
    return call(
        last_kernel, [((1, 1, 1, atoms), F32), ((3, 1, 1, 1, atoms), F32)], exchange(rows)
    )


def solution(mesh):
    cell = P("gx", "gy", "gz")
    in_specs = (
        P(None, "gx", "gy", "gz", None),
        P("gx", "gy", "gz", None),
        cell,
        cell,
        P("gx", "gy", "gz", None),
        P("gx", "gy", "gz", None),
        P(None, "gx", "gy", "gz", None),
    ) + (P(),) * 9
    out_specs = (P("gx", "gy", "gz", None), P(None, "gx", "gy", "gz", None))
    return jax.shard_map(local, mesh=mesh, in_specs=in_specs, out_specs=out_specs, check_vma=False)
```
